1024 devices in a mesh: dp: 64 (over z, x_hi), tensor: 16 (over x_lo, y, core).
Axes of the slice: x: 4 (x_hi: 2, x_lo: 2; x = x_hi * 2 + x_lo), y: 4, z: 32, core: 2. Of those that a mesh axis runs over, the one named last changes fastest.
Arguments:
- activations: bfloat16 [384, 8192], P('dp', 'tensor'), may hold values from -6 to 6
- cotangent: bfloat16 [384, 8192], P('dp', 'tensor'), may hold values from -6 to 6
- w_gate: bfloat16 [28672, 8192], P('dp', 'tensor'), may hold values from -0.0625 to 0.0625
- w_up: bfloat16 [28672, 8192], P('dp', 'tensor'), may hold values from -0.0625 to 0.0625
- w_down: bfloat16 [28672, 8192], P('dp', 'tensor'), may hold values from -0.03125 to 0.03125
Outputs:
- output: bfloat16 [384, 8192], P('dp', 'tensor')
- grad_input: bfloat16 [384, 8192], P('dp', 'tensor')
- grad_gate: bfloat16 [28672, 8192], P('dp', 'tensor')
- grad_up: bfloat16 [28672, 8192], P('dp', 'tensor')
- grad_down: bfloat16 [28672, 8192], P('dp', 'tensor')
The draws below stay inside these ranges and needn't reach their ends.
All inputs are finite; a program needn't handle non-finite values.
Results may differ from the reference program's by a relative error of at most 0.0049.
Values may be sent and summed in bfloat16 or wider, within the bound.
A program may use at most 32 MiB of HBM per device.

```python
import jax
import jax.numpy as jnp

D = 8192
FF = 28672
TOKENS = 384


def levels(key, dims, cuts, smallest, top_value):
    gain = 1.0
    for axis_at, blocks in cuts:
        heights = jax.random.uniform(jax.random.fold_in(jax.random.fold_in(key, 6), axis_at), (blocks,), jnp.float32, smallest / len(cuts), top_value / len(cuts))
        gain = gain * jnp.repeat(jnp.exp(heights), dims[axis_at] // blocks).reshape((-1,) + (1,) * (len(dims) - 1 - axis_at))
    return gain


def bell_draw(key, shape, spread, reach, pieces=(), dtype=jnp.bfloat16):
    factor_of = levels(key, shape, pieces, -0.22, 0.18) if pieces else 1.0
    values = jax.random.normal(key, shape, jnp.float32) * spread * factor_of
    return jnp.minimum(jnp.maximum(values, -reach), reach).astype(dtype)


def setup_inputs(seed: int = 0) -> dict:
    key_of = jax.random.split(jax.random.key(seed), 6)
    return {
        "activations": bell_draw(key_of[0], (TOKENS, D), 1.0, 6.0, ((0, 64), (1, 16))),
        "cotangent": bell_draw(key_of[1], (TOKENS, D), 1.0, 6.0, ((0, 64), (1, 16))),
        "w_gate": bell_draw(key_of[2], (FF, D), D ** -0.5, 0.0625, ((0, 64), (1, 16))),
        "w_up": bell_draw(key_of[3], (FF, D), D ** -0.5, 0.0625, ((0, 64), (1, 16))),
        "w_down": bell_draw(key_of[4], (FF, D), FF ** -0.5, 0.03125, ((0, 64), (1, 16))),
    }


def reference(activations, cotangent, w_gate, w_up, w_down):
    gate_sums = jnp.dot(activations, w_gate.T, preferred_element_type=jnp.float32)
    up_sums = jnp.dot(activations, w_up.T, preferred_element_type=jnp.float32)
    grad_hidden = jnp.dot(cotangent, w_down.T, preferred_element_type=jnp.float32)
    sigmoid_gate = jax.nn.sigmoid(gate_sums)
    silu_gate = gate_sums * sigmoid_gate
    hidden = (silu_gate * up_sums).astype(jnp.bfloat16)
    d_up = (grad_hidden * silu_gate).astype(jnp.bfloat16)
    d_gate = (grad_hidden * up_sums * sigmoid_gate * (1.0 + gate_sums * (1.0 - sigmoid_gate))).astype(jnp.bfloat16)
    output = jnp.dot(hidden, w_down, preferred_element_type=jnp.float32).astype(jnp.bfloat16)
    grad_input = (jnp.dot(d_gate, w_gate, preferred_element_type=jnp.float32)
                  + jnp.dot(d_up, w_up, preferred_element_type=jnp.float32)).astype(jnp.bfloat16)
    grad_gate = jnp.dot(d_gate.T, activations, preferred_element_type=jnp.float32).astype(jnp.bfloat16)
    grad_up = jnp.dot(d_up.T, activations, preferred_element_type=jnp.float32).astype(jnp.bfloat16)
    grad_down = jnp.dot(hidden.T, cotangent, preferred_element_type=jnp.float32).astype(jnp.bfloat16)
    return (output, grad_input, grad_gate, grad_up, grad_down)
```

```python
import functools

import jax
import jax.numpy as jnp
import numpy as np
from jax import lax
from jax.experimental import pallas as pl
from jax.experimental.pallas import tpu as pltpu
from jax.sharding import PartitionSpec as P

MESH = pl.DeviceIdType.MESH
F32 = jnp.float32
BF16 = jnp.bfloat16

NEAR = (0, 1, -1, 2, -2, 3, -3, 4)
FAR = (0, 8, -8, 16)
TOK = 6
QUARTERS = 4
ROWS = 2 * TOK * QUARTERS
GROUP = TOK * len(NEAR)
N_COPIES = 160


def selections():
    fold = np.zeros((QUARTERS, ROWS, 16), np.float32)
    unfold = np.zeros((QUARTERS, 2 * GROUP, 8 * ROWS), np.float32)
    last = np.zeros((QUARTERS, 16, ROWS), np.float32)
    for q in range(QUARTERS):
        for a in range(2):
            for t in range(TOK):
                row = q * 2 * TOK + a * TOK + t
                fold[q, row, a * 8 + t] = 1
                last[q, a * 8 + t, row] = 1
                for w in range(8):
                    unfold[q, a * GROUP + w * TOK + t, w * ROWS + row] = 1
    back = np.transpose(unfold, (0, 2, 1))
    return [jnp.asarray(v, BF16) for v in (fold, unfold, back, last)]


def dot(a, b):
    return lax.dot_general(a, b, (((1,), (0,)), ((), ())), preferred_element_type=F32)


def dot_t(a, b):
    return lax.dot_general(a, b, (((1,), (1,)), ((), ())), preferred_element_type=F32)


def t_dot(a, b):
    return lax.dot_general(a, b, (((0,), (0,)), ((), ())), preferred_element_type=F32)


def kernel(
    zs, act_ref, cot_ref, wg_hbm, wu_hbm, wd_hbm, fold_ref, unfold_hbm, back_hbm, last_ref,
    out_ref, gin_ref, gg_ref, gu_ref, gd_ref,
    wg, wu, wd, unfold, back, stage16, g_buf, acts, cots,
    pa, pb, ra, rb, qa, qb, a1, b1, sa, sb, a2, b2, ha, hb, hd,
    own_sum, xs, xr_buf, rbuf, rw, rw7a, rw7b, fsend, frecv,
    local_sem, send_sem, recv_sem,
):
    dp, tn = lax.axis_index("dp"), lax.axis_index("tensor")
    z, xh = dp // 2, dp % 2
    xl, y, c = tn // 8, (tn // 2) % 4, tn % 2
    xo, co = 1 - xl, 1 - c

    def z_dev(d):
        return (((z + (d + zs)) % zs) * 2 + xh, tn)

    def t_dev(x_, y_, c_):
        return (dp, (x_ * 4 + y_) * 2 + c_)

    def y_at(d):
        return (y + d) % 4

    x2_dev = (z * 2 + (1 - xh), tn)
    x1_dev = t_dev(xo, y, c)
    c_dev = t_dev(xl, y, co)

    loads = []
    for i, (s, d) in enumerate(
        ((wg_hbm, wg), (wu_hbm, wu), (wd_hbm, wd), (unfold_hbm, unfold), (back_hbm, back))
    ):
        cp = pltpu.make_async_copy(s, d, local_sem.at[i])
        cp.start()
        loads.append(cp)

    barrier = pltpu.get_barrier_semaphore()
    peers = [z_dev(d) for d in (8, -8, 4, -4, 3, -3, 2, -2, 1, -1)]
    peers += [x2_dev, x1_dev, c_dev] + [t_dev(xl, y_at(d), c) for d in (1, 2, 3)]
    for peer in peers:
        pl.semaphore_signal(barrier, inc=1, device_id=peer, device_id_type=MESH)

    sent = []

    def send(src, dst, dev):
        i = len(sent)
        cp = pltpu.make_async_remote_copy(
            src_ref=src, dst_ref=dst, send_sem=send_sem.at[i], recv_sem=recv_sem.at[i],
            device_id=dev, device_id_type=MESH,
        )
        cp.start()
        sent.append(cp)
        return cp

    stage16[...] = jnp.zeros_like(stage16)
    stage16[0:TOK] = act_ref[...].astype(F32)
    stage16[8 : 8 + TOK] = cot_ref[...].astype(F32)
    raw = stage16[...].astype(BF16)
    block = jnp.zeros((ROWS, 128), F32)
    for q in range(QUARTERS):
        block += dot(fold_ref[q], raw[:, q * 128 : (q + 1) * 128])
    g_buf[0, 0, 0] = block.astype(BF16)

    pl.semaphore_wait(barrier, len(peers))

    far = {}
    far[2] = send(g_buf.at[0, 0, 0], g_buf.at[0, 2, 0], z_dev(8))
    far[1] = send(g_buf.at[0, 0, 0], g_buf.at[0, 1, 0], z_dev(-8))
    near = {}

    def spread(f):
        for w in range(1, 7):
            near[f, w] = send(g_buf.at[0, f, 0], g_buf.at[0, f, w], z_dev(-NEAR[w]))
        if f in (0, 1):
            near[f, 7] = send(g_buf.at[0, f, 0], g_buf.at[0, f, 7], z_dev(-4))
        if f in (0, 2):
            near[2 if f == 0 else 3, 7] = send(
                g_buf.at[0, f, 0], g_buf.at[0, 2 if f == 0 else 3, 7], z_dev(4)
            )

    across = {}

    def cross(f):
        for w in range(1, 8):
            near[f, w].wait_recv()
        across[f] = send(g_buf.at[0, f], g_buf.at[1, f], x2_dev)

    def order(x, f):
        blocks = g_buf[x, f].reshape(8 * ROWS, 128)
        for q in range(QUARTERS):
            rows = dot(unfold[q], blocks).astype(BF16)
            lanes = slice(q * 128, (q + 1) * 128)
            acts[x, f, :, lanes] = rows[:GROUP]
            cots[x, f, :, lanes] = rows[GROUP:]

    spread(0)
    far[2].wait_recv()
    far[3] = send(g_buf.at[0, 2, 0], g_buf.at[0, 3, 0], z_dev(8))
    spread(2)
    far[1].wait_recv()
    spread(1)
    for cp in loads:
        cp.wait()
    cross(0)
    order(0, 0)
    far[3].wait_recv()
    spread(3)
    cross(1)
    cross(2)
    order(0, 1)
    order(0, 2)
    across[0].wait_recv()
    order(1, 0)
    cross(3)
    order(0, 3)

    pair = {}

    def partial_sums(x):
        a_rows = acts[x].reshape(4 * GROUP, 512)
        c_rows = cots[x].reshape(4 * GROUP, 512)
        for j, (rows, weight) in enumerate(((a_rows, wg), (a_rows, wu), (c_rows, wd))):
            part = slice(j * GROUP, (j + 1) * GROUP)
            low = dot_t(rows, weight[0:256])
            high = dot_t(rows, weight[256:448])
            for f in range(4):
                r = slice(f * GROUP, (f + 1) * GROUP)
                pa[0, f, x, part] = low[r, 0:128]
                pb[0, x, f, part] = low[r, 128:256]
                pa[1, f, x, part] = high[r, 0:128]
                pb[1, x, f, part, 0:64] = high[r, 128:192]
                pb[1, x, f, part, 64:128] = jnp.zeros((GROUP, 64), F32)
        pair[x, 0] = send(pa.at[co, :, x], ra.at[:, x], c_dev)
        pair[x, 1] = send(pb.at[co, x], rb.at[x], c_dev)

    partial_sums(0)
    for f in (1, 2, 3):
        across[f].wait_recv()
        order(1, f)
    partial_sums(1)

    pair[0, 1].wait_recv()
    pair[1, 1].wait_recv()
    qb[...] = pb[c] + rb[...]
    first_b = send(qb.at[xo], b1, x1_dev)
    pair[0, 0].wait_recv()
    pair[1, 0].wait_recv()
    qa[...] = pa[c] + ra[...]
    first_a = [send(qa.at[y_at(d)], a1.at[d - 1], t_dev(xl, y_at(d), c)) for d in (2, 1, 3)]
    first_b.wait_recv()
    sb[...] = qb[xl] + b1[...]
    second_b = [send(sb.at[y_at(d)], b2.at[d - 1], t_dev(xl, y_at(d), c)) for d in (2, 1, 3)]
    for cp in first_a:
        cp.wait_recv()
    sa[...] = qa[y] + a1[0] + a1[1] + a1[2]
    second_a = send(sa.at[xo], a2, x1_dev)

    def finish(sums):
        gate, up, grad = sums[0:GROUP], sums[GROUP : 2 * GROUP], sums[2 * GROUP : 3 * GROUP]
        s = jax.nn.sigmoid(gate)
        silu = gate * s
        hidden = (silu * up).astype(BF16)
        d_gate = (grad * up * s * (1.0 + gate * (1.0 - s))).astype(BF16)
        d_up = (grad * silu).astype(BF16)
        return jnp.concatenate([hidden, d_gate, d_up], axis=0)

    y_peers = [(d, t_dev(xl, y_at(d), c)) for d in (2, 1, 3)]
    cores = []
    second_a.wait_recv()
    ha[c, y, xl] = finish(sa[xl] + a2[...])
    near_a = send(ha.at[c, y, xl], ha.at[c, y, xl], x1_dev)
    for cp in second_b:
        cp.wait_recv()
    hb[c, xl, y] = finish(sb[y] + b2[0] + b2[1] + b2[2])
    near_b = [send(hb.at[c, xl, y], hb.at[c, xl, y], dev) for d, dev in y_peers]
    near_a.wait_recv()
    wide_a = [send(ha.at[c, y], ha.at[c, y], dev) for d, dev in y_peers]
    cores.append(send(ha.at[c, y], ha.at[c, y], c_dev))
    for cp in near_b:
        cp.wait_recv()
    wide_b = send(hb.at[c, xl], hb.at[c, xl], x1_dev)
    cores.append(send(hb.at[c, xl], hb.at[c, xl], c_dev))
    for (d, dev), cp in zip(y_peers, wide_a):
        cp.wait_recv()
        cores.append(send(ha.at[c, y_at(4 - d)], ha.at[c, y_at(4 - d)], c_dev))
    wide_b.wait_recv()
    cores.append(send(hb.at[c, xo], hb.at[c, xo], c_dev))
    for cp in cores:
        cp.wait_recv()

    for j in range(3):
        part = slice(j * GROUP, (j + 1) * GROUP)
        for half in range(2):
            for x in range(2):
                for f in range(4):
                    hd[j, x, f, :, half * 256 : half * 256 + 128] = ha[half, f, x, part]
                    hd[j, x, f, :, half * 256 + 128 : half * 256 + 256] = hb[half, x, f, part]

    def hidden_sums(x):
        h, dg, du = [hd[j, x].reshape(4 * GROUP, 512)[:, :448] for j in range(3)]
        return dot(h, wd[...]), dot(dg, wg[...]) + dot(du, wu[...])

    f_order = (3, 2, 1, 0)
    fwd, bwd = hidden_sums(1)
    over = {}
    for f in f_order:
        r = slice(f * GROUP, (f + 1) * GROUP)
        xs[f, 0:GROUP] = fwd[r].astype(BF16)
        xs[f, GROUP : 2 * GROUP] = bwd[r].astype(BF16)
        over[f] = send(xs.at[f], xr_buf.at[f], x2_dev)
    fwd, bwd = hidden_sums(0)
    for f in f_order:
        r = slice(f * GROUP, (f + 1) * GROUP)
        own_sum[f, 0:GROUP] = fwd[r]
        own_sum[f, GROUP : 2 * GROUP] = bwd[r]

    step3, step0 = {}, {}
    for f in f_order:
        over[f].wait_recv()
        both = (own_sum[f] + xr_buf[f].astype(F32)).astype(BF16)
        rows = jnp.zeros((8 * ROWS, 128), F32)
        for q in range(QUARTERS):
            rows += dot(back[q], both[:, q * 128 : (q + 1) * 128])
        rows = rows.astype(BF16)
        for w in range(8):
            rbuf[w, f] = rows[w * ROWS : (w + 1) * ROWS]
        if f == 3:
            for w in range(1, 7):
                step3[w] = send(rbuf.at[w, 3], rw.at[w, 3], z_dev(NEAR[w]))
        if f == 2:
            minus4 = send(rbuf.at[7, pl.ds(2, 2)], rw7b, z_dev(-4))
    for w in range(1, 7):
        step0[w] = send(rbuf.at[w, pl.ds(0, 3)], rw.at[w, pl.ds(0, 3)], z_dev(NEAR[w]))
    plus4 = send(rbuf.at[7, pl.ds(0, 2)], rw7a, z_dev(4))

    def near_sum(f):
        total = rbuf[0, f].astype(F32)
        for w in range(1, 7):
            total += rw[w, f].astype(F32)
        return total

    for w in range(1, 7):
        step3[w].wait_recv()
    fsend[0] = near_sum(3).astype(BF16)
    far16 = send(fsend.at[0], frecv.at[0], z_dev(8))

    for w in range(1, 7):
        step0[w].wait_recv()
    minus4.wait_recv()
    plus4.wait_recv()
    fsend[1] = (near_sum(2) + rw7b[1].astype(F32)).astype(BF16)
    back8 = send(fsend.at[1], frecv.at[1], z_dev(-8))

    a_all = acts[...].reshape(8 * GROUP, 512)
    c_all = cots[...].reshape(8 * GROUP, 512)

    def weight_grad(j, rows, ref):
        d = hd[j].reshape(8 * GROUP, 512)
        ref[0:256] = t_dot(d[:, 0:256], rows).astype(BF16)
        ref[256:448] = t_dot(d[:, 256:448], rows).astype(BF16)

    weight_grad(1, a_all, gg_ref)
    weight_grad(2, a_all, gu_ref)
    far16.wait_recv()
    fsend[2] = (near_sum(1) + rw7a[1].astype(F32) + frecv[0].astype(F32)).astype(BF16)
    on8 = send(fsend.at[2], frecv.at[2], z_dev(8))
    weight_grad(0, c_all, gd_ref)

    total = near_sum(0) + rw7a[0].astype(F32) + rw7b[0].astype(F32)
    back8.wait_recv()
    total += frecv[1].astype(F32)
    on8.wait_recv()
    total = (total + frecv[2].astype(F32)).astype(BF16)
    for q in range(QUARTERS):
        stage16[:, q * 128 : (q + 1) * 128] = dot(last_ref[q], total)
    out_ref[...] = stage16[0:TOK].astype(BF16)
    gin_ref[...] = stage16[8 : 8 + TOK].astype(BF16)
    for cp in sent:
        cp.wait_send()


def on_device(zs, activations, cotangent, w_gate, w_up, w_down):
    tokens, features = activations.shape
    hidden = w_gate.shape[0]
    fold, unfold, back, last = selections()
    vmem = pl.BlockSpec(memory_space=pltpu.VMEM)
    anywhere = pl.BlockSpec(memory_space=pl.ANY)
    weight = (hidden, features)
    row3 = 3 * GROUP
    scratch = [
        pltpu.VMEM(weight, BF16), pltpu.VMEM(weight, BF16), pltpu.VMEM(weight, BF16),
        pltpu.VMEM(unfold.shape, BF16), pltpu.VMEM(back.shape, BF16),
        pltpu.VMEM((16, features), F32),
        pltpu.VMEM((2, 4, 8, ROWS, 128), BF16),
        pltpu.VMEM((2, 4, GROUP, features), BF16), pltpu.VMEM((2, 4, GROUP, features), BF16),
        pltpu.VMEM((2, 4, 2, row3, 128), F32), pltpu.VMEM((2, 2, 4, row3, 128), F32),
        pltpu.VMEM((4, 2, row3, 128), F32), pltpu.VMEM((2, 4, row3, 128), F32),
        pltpu.VMEM((4, 2, row3, 128), F32), pltpu.VMEM((2, 4, row3, 128), F32),
        pltpu.VMEM((3, 2, row3, 128), F32), pltpu.VMEM((4, row3, 128), F32),
        pltpu.VMEM((2, row3, 128), F32), pltpu.VMEM((4, row3, 128), F32),
        pltpu.VMEM((row3, 128), F32), pltpu.VMEM((3, row3, 128), F32),
        pltpu.VMEM((2, 4, 2, row3, 128), BF16), pltpu.VMEM((2, 2, 4, row3, 128), BF16),
        pltpu.VMEM((3, 2, 4, GROUP, 512), BF16),
        pltpu.VMEM((4, 2 * GROUP, features), F32),
        pltpu.VMEM((4, 2 * GROUP, features), BF16), pltpu.VMEM((4, 2 * GROUP, features), BF16),
        pltpu.VMEM((8, 4, ROWS, 128), BF16), pltpu.VMEM((8, 4, ROWS, 128), BF16),
        pltpu.VMEM((2, ROWS, 128), BF16), pltpu.VMEM((2, ROWS, 128), BF16),
        pltpu.VMEM((3, ROWS, 128), BF16), pltpu.VMEM((3, ROWS, 128), BF16),
        pltpu.SemaphoreType.DMA((5,)),
        pltpu.SemaphoreType.DMA((N_COPIES,)), pltpu.SemaphoreType.DMA((N_COPIES,)),
    ]
    block = jax.ShapeDtypeStruct((tokens, features), BF16)
    grad = jax.ShapeDtypeStruct(weight, BF16)
    return pl.pallas_call(
        functools.partial(kernel, zs),
        out_shape=(block, block, grad, grad, grad),
        in_specs=[vmem, vmem, anywhere, anywhere, anywhere, vmem, anywhere, anywhere, vmem],
        out_specs=(vmem,) * 5,
        scratch_shapes=scratch,
        compiler_params=pltpu.CompilerParams(
            collective_id=0, has_side_effects=True, vmem_limit_bytes=56 * 2**20
        ),
        cost_estimate=pl.CostEstimate(
            flops=18 * 384 * hidden * features, bytes_accessed=12 * hidden * features,
            transcendentals=0,
        ),
        name="ffn",
    )(activations, cotangent, w_gate, w_up, w_down, fold, unfold, back, last)


def solution(mesh):
    spec = P("dp", "tensor")
    return jax.shard_map(
        functools.partial(on_device, mesh.shape["dp"] // 2),
        mesh=mesh,
        in_specs=(spec,) * 5,
        out_specs=(spec,) * 5,
        check_vma=False,
    )
```

```python
import functools

import jax
import jax.numpy as jnp
import numpy as np
from jax import lax
from jax.experimental import pallas as pl
from jax.experimental.pallas import tpu as pltpu
from jax.sharding import PartitionSpec as P

MESH = pl.DeviceIdType.MESH
F32 = jnp.float32
BF16 = jnp.bfloat16

NEAR = (0, 1, -1, 2)
FAR = (0, 4, -4, 8, -8, 12, -12, 16)
F0, P4, M4, P8, M8, P12, M12, F16 = range(8)
ABOVE = (F0, P4, P8, P12)
BELOW = {M4: F0, M8: M4, M12: M8, F16: M12}
TOK = 6
QUARTERS = 4
ROWS = 2 * TOK * QUARTERS
BLOCKS = 8
GROUP = TOK * BLOCKS
N_COPIES = 160


def selections():
    fold = np.zeros((QUARTERS, ROWS, 16), np.float32)
    unfold = np.zeros((QUARTERS, 2 * GROUP, 8 * ROWS), np.float32)
    last = np.zeros((QUARTERS, 16, ROWS), np.float32)
    for q in range(QUARTERS):
        for a in range(2):
            for t in range(TOK):
                row = q * 2 * TOK + a * TOK + t
                fold[q, row, a * 8 + t] = 1
                last[q, a * 8 + t, row] = 1
                for w in range(8):
                    unfold[q, a * GROUP + w * TOK + t, w * ROWS + row] = 1
    back = np.transpose(unfold, (0, 2, 1))
    return [jnp.asarray(v, BF16) for v in (fold, unfold, back, last)]


def dot(a, b):
    return lax.dot_general(a, b, (((1,), (0,)), ((), ())), preferred_element_type=F32)


def dot_t(a, b):
    return lax.dot_general(a, b, (((1,), (1,)), ((), ())), preferred_element_type=F32)


def t_dot(a, b):
    return lax.dot_general(a, b, (((0,), (0,)), ((), ())), preferred_element_type=F32)


def kernel(
    zs, act_ref, cot_ref, wg_hbm, wu_hbm, wd_hbm, fold_ref, unfold_hbm, back_hbm, last_ref,
    out_ref, gin_ref, gg_ref, gu_ref, gd_ref,
    wg, wu, wd, unfold, back, stage16, g_buf, acts, cots,
    pa, pb, ra, rb, qa, qb, a1, b1, sa, sb, a2, b2, ha, hb, hd,
    own_sum, xs, xr_buf, rbuf, rw, fsend, frecv,
    local_sem, send_sem, recv_sem,
):
    dp, tn = lax.axis_index("dp"), lax.axis_index("tensor")
    z, xh = dp // 2, dp % 2
    xl, y, c = tn // 8, (tn // 2) % 4, tn % 2
    xo, co = 1 - xl, 1 - c

    def z_dev(d):
        return (((z + (d + zs)) % zs) * 2 + xh, tn)

    def t_dev(x_, y_, c_):
        return (dp, (x_ * 4 + y_) * 2 + c_)

    def y_at(d):
        return (y + d) % 4

    x2_dev = (z * 2 + (1 - xh), tn)
    x1_dev = t_dev(xo, y, c)
    c_dev = t_dev(xl, y, co)

    loads = []
    for i, (s, d) in enumerate(
        ((wg_hbm, wg), (wu_hbm, wu), (wd_hbm, wd), (unfold_hbm, unfold), (back_hbm, back))
    ):
        cp = pltpu.make_async_copy(s, d, local_sem.at[i])
        cp.start()
        loads.append(cp)

    barrier = pltpu.get_barrier_semaphore()
    peers = [z_dev(d) for d in (8, -8, 4, -4, 2, -2, 1, -1)]
    peers += [x2_dev, x1_dev, c_dev] + [t_dev(xl, y_at(d), c) for d in (1, 2, 3)]
    for peer in peers:
        pl.semaphore_signal(barrier, inc=1, device_id=peer, device_id_type=MESH)

    sent = []

    def send(src, dst, dev):
        i = len(sent)
        cp = pltpu.make_async_remote_copy(
            src_ref=src, dst_ref=dst, send_sem=send_sem.at[i], recv_sem=recv_sem.at[i],
            device_id=dev, device_id_type=MESH,
        )
        cp.start()
        sent.append(cp)
        return cp

    stage16[...] = jnp.zeros_like(stage16)
    stage16[0:TOK] = act_ref[...].astype(F32)
    stage16[8 : 8 + TOK] = cot_ref[...].astype(F32)
    raw = stage16[...].astype(BF16)
    block = jnp.zeros((ROWS, 128), F32)
    for q in range(QUARTERS):
        block += dot(fold_ref[q], raw[:, q * 128 : (q + 1) * 128])
    g_buf[0, 0, 0] = block.astype(BF16)

    pl.semaphore_wait(barrier, len(peers))

    own = g_buf.at[0, F0, 0]
    far = {}
    far[M8] = send(own, g_buf.at[0, M8, 0], z_dev(8))
    far[P8] = send(own, g_buf.at[0, P8, 0], z_dev(-8))
    far[M4] = send(own, g_buf.at[0, M4, 0], z_dev(4))
    far[P4] = send(own, g_buf.at[0, P4, 0], z_dev(-4))
    near, across = {}, {}

    def spread(f):
        block = g_buf.at[0, f, 0]
        near[f, 1] = send(block, g_buf.at[0, f, 1], z_dev(-1))
        near[f, 2] = send(block, g_buf.at[0, f, 2], z_dev(1))
        if f in ABOVE:
            near[f, 3] = send(block, g_buf.at[0, f, 3], z_dev(-2))
        for slot, source in BELOW.items():
            if source == f:
                near[slot, 3] = send(block, g_buf.at[0, slot, 3], z_dev(2))

    def cross(f):
        for w in (1, 2, 3):
            near[f, w].wait_recv()
        across[f] = send(g_buf.at[0, f], g_buf.at[1, f], x2_dev)

    def order(x, g):
        blocks = g_buf[x, 2 * g : 2 * g + 2].reshape(BLOCKS * ROWS, 128)
        for q in range(QUARTERS):
            rows = dot(unfold[q], blocks).astype(BF16)
            lanes = slice(q * 128, (q + 1) * 128)
            acts[x, g, :, lanes] = rows[:GROUP]
            cots[x, g, :, lanes] = rows[GROUP:]

    def order_other(g):
        across[2 * g].wait_recv()
        across[2 * g + 1].wait_recv()
        order(1, g)

    spread(F0)
    far[P4].wait_recv()
    spread(P4)
    far[M4].wait_recv()
    spread(M4)
    far[M8].wait_recv()
    far[F16] = send(g_buf.at[0, M8, 0], g_buf.at[0, F16, 0], z_dev(8))
    far[M12] = send(g_buf.at[0, M8, 0], g_buf.at[0, M12, 0], z_dev(4))
    far[P8].wait_recv()
    far[P12] = send(g_buf.at[0, P8, 0], g_buf.at[0, P12, 0], z_dev(-4))
    spread(P8)
    spread(M8)
    cross(F0)
    cross(P4)
    cross(M4)
    for cp in loads:
        cp.wait()
    order(0, 0)
    cross(P8)
    cross(M8)
    far[M12].wait_recv()
    spread(M12)
    far[P12].wait_recv()
    spread(P12)
    order(0, 1)
    far[F16].wait_recv()
    spread(F16)
    cross(P12)
    cross(M12)
    order(0, 2)
    cross(F16)
    order(0, 3)

    pair = {}

    def partial_sums(x):
        a_rows = acts[x].reshape(4 * GROUP, 512)
        c_rows = cots[x].reshape(4 * GROUP, 512)
        for j, (rows, weight) in enumerate(((a_rows, wg), (a_rows, wu), (c_rows, wd))):
            part = slice(j * GROUP, (j + 1) * GROUP)
            low = dot_t(rows, weight[0:256])
            high = dot_t(rows, weight[256:448])
            for f in range(4):
                r = slice(f * GROUP, (f + 1) * GROUP)
                pa[0, f, x, part] = low[r, 0:128]
                pb[0, x, f, part] = low[r, 128:256]
                pa[1, f, x, part] = high[r, 0:128]
                pb[1, x, f, part, 0:64] = high[r, 128:192]
                pb[1, x, f, part, 64:128] = jnp.zeros((GROUP, 64), F32)
        pair[x, 0] = send(pa.at[co, :, x], ra.at[:, x], c_dev)
        pair[x, 1] = send(pb.at[co, x], rb.at[x], c_dev)

    partial_sums(0)
    for g in range(4):
        order_other(g)
    partial_sums(1)

    pair[0, 1].wait_recv()
    pair[1, 1].wait_recv()
    qb[...] = pb[c] + rb[...]
    first_b = send(qb.at[xo], b1, x1_dev)
    pair[0, 0].wait_recv()
    pair[1, 0].wait_recv()
    qa[...] = pa[c] + ra[...]
    first_a = [send(qa.at[y_at(d)], a1.at[d - 1], t_dev(xl, y_at(d), c)) for d in (2, 1, 3)]
    first_b.wait_recv()
    sb[...] = qb[xl] + b1[...]
    second_b = [send(sb.at[y_at(d)], b2.at[d - 1], t_dev(xl, y_at(d), c)) for d in (2, 1, 3)]
    for cp in first_a:
        cp.wait_recv()
    sa[...] = qa[y] + a1[0] + a1[1] + a1[2]
    second_a = send(sa.at[xo], a2, x1_dev)

    def finish(sums):
        gate, up, grad = sums[0:GROUP], sums[GROUP : 2 * GROUP], sums[2 * GROUP : 3 * GROUP]
        s = jax.nn.sigmoid(gate)
        silu = gate * s
        hidden = (silu * up).astype(BF16)
        d_gate = (grad * up * s * (1.0 + gate * (1.0 - s))).astype(BF16)
        d_up = (grad * silu).astype(BF16)
        return jnp.concatenate([hidden, d_gate, d_up], axis=0)

    y_peers = [(d, t_dev(xl, y_at(d), c)) for d in (2, 1, 3)]
    cores = []
    second_a.wait_recv()
    ha[c, y, xl] = finish(sa[xl] + a2[...])
    near_a = send(ha.at[c, y, xl], ha.at[c, y, xl], x1_dev)
    for cp in second_b:
        cp.wait_recv()
    hb[c, xl, y] = finish(sb[y] + b2[0] + b2[1] + b2[2])
    near_b = [send(hb.at[c, xl, y], hb.at[c, xl, y], dev) for d, dev in y_peers]
    near_a.wait_recv()
    wide_a = [send(ha.at[c, y], ha.at[c, y], dev) for d, dev in y_peers]
    cores.append(send(ha.at[c, y], ha.at[c, y], c_dev))
    for cp in near_b:
        cp.wait_recv()
    wide_b = send(hb.at[c, xl], hb.at[c, xl], x1_dev)
    cores.append(send(hb.at[c, xl], hb.at[c, xl], c_dev))
    for (d, dev), cp in zip(y_peers, wide_a):
        cp.wait_recv()
        cores.append(send(ha.at[c, y_at(4 - d)], ha.at[c, y_at(4 - d)], c_dev))
    wide_b.wait_recv()
    cores.append(send(hb.at[c, xo], hb.at[c, xo], c_dev))
    for cp in cores:
        cp.wait_recv()

    for j in range(3):
        part = slice(j * GROUP, (j + 1) * GROUP)
        for half in range(2):
            for x in range(2):
                for f in range(4):
                    hd[j, x, f, :, half * 256 : half * 256 + 128] = ha[half, f, x, part]
                    hd[j, x, f, :, half * 256 + 128 : half * 256 + 256] = hb[half, x, f, part]

    def hidden_sums(x):
        h, dg, du = [hd[j, x].reshape(4 * GROUP, 512)[:, :448] for j in range(3)]
        return dot(h, wd[...]), dot(dg, wg[...]) + dot(du, wu[...])

    over = {}

    def give(g):
        over[g] = send(xs.at[g], xr_buf.at[g], x2_dev)

    fwd, bwd = hidden_sums(1)
    for g in range(4):
        r = slice(g * GROUP, (g + 1) * GROUP)
        xs[g, 0:GROUP] = fwd[r].astype(BF16)
        xs[g, GROUP : 2 * GROUP] = bwd[r].astype(BF16)
    give(3)
    give(2)
    fwd, bwd = hidden_sums(0)
    give(1)
    give(0)
    for g in range(4):
        r = slice(g * GROUP, (g + 1) * GROUP)
        own_sum[g, 0:GROUP] = fwd[r]
        own_sum[g, GROUP : 2 * GROUP] = bwd[r]

    part_in = {}

    def collect(g):
        over[g].wait_recv()
        both = (own_sum[g] + xr_buf[g].astype(F32)).astype(BF16)
        rows = jnp.zeros((BLOCKS * ROWS, 128), F32)
        for q in range(QUARTERS):
            rows += dot(back[q], both[:, q * 128 : (q + 1) * 128])
        rows = rows.astype(BF16)
        for i in range(BLOCKS):
            rbuf[2 * g + i // 4, i % 4] = rows[i * ROWS : (i + 1) * ROWS]
        for f in (2 * g + 1, 2 * g):
            part_in[f, 0] = send(rbuf.at[f, 1], rw.at[f, 0], z_dev(1))
            part_in[f, 1] = send(rbuf.at[f, 2], rw.at[f, 1], z_dev(-1))
            if f in ABOVE:
                part_in[f, 2] = send(rbuf.at[f, 3], rw.at[f, 2], z_dev(2))
            else:
                part_in[BELOW[f], 3] = send(rbuf.at[f, 3], rw.at[BELOW[f], 3], z_dev(-2))

    def near_sum(f):
        total = rbuf[f, 0].astype(F32)
        for i in range(4):
            if (f, i) in part_in:
                part_in[f, i].wait_recv()
                total += rw[f, i].astype(F32)
        return total

    onward = {}

    def pass_on(i, f, dev, *others):
        total = near_sum(f)
        for o in others:
            onward[o].wait_recv()
            total += frecv[o].astype(F32)
        fsend[i] = total.astype(BF16)
        onward[i] = send(fsend.at[i], frecv.at[i], dev)

    collect(3)
    collect(2)
    pass_on(0, F16, z_dev(8))
    collect(1)
    pass_on(2, M12, z_dev(-4))
    pass_on(1, P12, z_dev(4))
    collect(0)
    pass_on(5, P4, z_dev(4))
    pass_on(6, M4, z_dev(-4))

    a_all = acts[...].reshape(8 * GROUP, 512)
    c_all = cots[...].reshape(8 * GROUP, 512)

    def weight_grad(j, rows, ref):
        d = hd[j].reshape(8 * GROUP, 512)
        ref[0:256] = t_dot(d[:, 0:256], rows).astype(BF16)
        ref[256:448] = t_dot(d[:, 256:448], rows).astype(BF16)

    weight_grad(1, a_all, gg_ref)
    pass_on(4, M8, z_dev(-8), 2)
    pass_on(3, P8, z_dev(8), 1, 0)
    weight_grad(2, a_all, gu_ref)
    weight_grad(0, c_all, gd_ref)

    total = near_sum(F0)
    for o in (5, 6, 4, 3):
        onward[o].wait_recv()
        total += frecv[o].astype(F32)
    total = total.astype(BF16)
    for q in range(QUARTERS):
        stage16[:, q * 128 : (q + 1) * 128] = dot(last_ref[q], total)
    out_ref[...] = stage16[0:TOK].astype(BF16)
    gin_ref[...] = stage16[8 : 8 + TOK].astype(BF16)
    for cp in sent:
        cp.wait_send()


def hand_over(*refs):
    sem = refs[-1]
    copies = [pltpu.make_async_copy(refs[i], refs[5 + i], sem.at[i]) for i in range(5)]
    for cp in copies:
        cp.start()
    for cp in copies:
        cp.wait()


def on_device(zs, activations, cotangent, w_gate, w_up, w_down):
    tokens, features = activations.shape
    hidden = w_gate.shape[0]
    fold, unfold, back, last = selections()
    vmem = pl.BlockSpec(memory_space=pltpu.VMEM)
    anywhere = pl.BlockSpec(memory_space=pl.ANY)
    weight = (hidden, features)
    row3 = 3 * GROUP
    scratch = [
        pltpu.VMEM(weight, BF16), pltpu.VMEM(weight, BF16), pltpu.VMEM(weight, BF16),
        pltpu.VMEM(unfold.shape, BF16), pltpu.VMEM(back.shape, BF16),
        pltpu.VMEM((16, features), F32),
        pltpu.VMEM((2, 8, 4, ROWS, 128), BF16),
        pltpu.VMEM((2, 4, GROUP, features), BF16), pltpu.VMEM((2, 4, GROUP, features), BF16),
        pltpu.VMEM((2, 4, 2, row3, 128), F32), pltpu.VMEM((2, 2, 4, row3, 128), F32),
        pltpu.VMEM((4, 2, row3, 128), F32), pltpu.VMEM((2, 4, row3, 128), F32),
        pltpu.VMEM((4, 2, row3, 128), F32), pltpu.VMEM((2, 4, row3, 128), F32),
        pltpu.VMEM((3, 2, row3, 128), F32), pltpu.VMEM((4, row3, 128), F32),
        pltpu.VMEM((2, row3, 128), F32), pltpu.VMEM((4, row3, 128), F32),
        pltpu.VMEM((row3, 128), F32), pltpu.VMEM((3, row3, 128), F32),
        pltpu.VMEM((2, 4, 2, row3, 128), BF16), pltpu.VMEM((2, 2, 4, row3, 128), BF16),
        pltpu.VMEM((3, 2, 4, GROUP, 512), BF16),
        pltpu.VMEM((4, 2 * GROUP, features), F32),
        pltpu.VMEM((4, 2 * GROUP, features), BF16), pltpu.VMEM((4, 2 * GROUP, features), BF16),
        pltpu.VMEM((8, 4, ROWS, 128), BF16), pltpu.VMEM((8, 4, ROWS, 128), BF16),
        pltpu.VMEM((7, ROWS, 128), BF16), pltpu.VMEM((7, ROWS, 128), BF16),
        pltpu.SemaphoreType.DMA((5,)),
        pltpu.SemaphoreType.DMA((N_COPIES,)), pltpu.SemaphoreType.DMA((N_COPIES,)),
    ]
    block = jax.ShapeDtypeStruct((tokens, features), BF16)
    grad = jax.ShapeDtypeStruct(weight, BF16)
    results = pl.pallas_call(
        functools.partial(kernel, zs),
        out_shape=(block, block, grad, grad, grad),
        in_specs=[vmem, vmem, anywhere, anywhere, anywhere, vmem, anywhere, anywhere, vmem],
        out_specs=(vmem,) * 5,
        scratch_shapes=scratch,
        compiler_params=pltpu.CompilerParams(
            collective_id=0, has_side_effects=True, vmem_limit_bytes=56 * 2**20
        ),
        cost_estimate=pl.CostEstimate(
            flops=18 * 384 * hidden * features, bytes_accessed=12 * hidden * features,
            transcendentals=0,
        ),
        name="ffn",
    )(activations, cotangent, w_gate, w_up, w_down, fold, unfold, back, last)
    return pl.pallas_call(
        hand_over,
        out_shape=(block, block, grad, grad, grad),
        in_specs=[vmem] * 5,
        out_specs=(anywhere,) * 5,
        scratch_shapes=[pltpu.SemaphoreType.DMA((5,))],
        name="hand_over",
    )(*results)


def solution(mesh):
    spec = P("dp", "tensor")
    return jax.shard_map(
        functools.partial(on_device, mesh.shape["dp"] // 2),
        mesh=mesh,
        in_specs=(spec,) * 5,
        out_specs=(spec,) * 5,
        check_vma=False,
    )
```

```python
import functools

import jax
import jax.numpy as jnp
import numpy as np
from jax import lax
from jax.experimental import pallas as pl
from jax.experimental.pallas import tpu as pltpu
from jax.sharding import PartitionSpec as P

MESH = pl.DeviceIdType.MESH
F32 = jnp.float32
BF16 = jnp.bfloat16

NEAR = (0, 1, -1, 2)
FAR = (0, 4, -4, 8, -8, 12, -12, 16)
F0, P4, M4, P8, M8, P12, M12, F16 = range(8)
ABOVE = (F0, P4, P8, P12)
BELOW = {M4: F0, M8: M4, M12: M8, F16: M12}
TOK = 6
QUARTERS = 4
ROWS = 2 * TOK * QUARTERS
BLOCKS = 8
GROUP = TOK * BLOCKS
N_COPIES = 160


def selections():
    fold = np.zeros((QUARTERS, ROWS, 16), np.float32)
    unfold = np.zeros((QUARTERS, 2 * GROUP, 8 * ROWS), np.float32)
    last = np.zeros((QUARTERS, 16, ROWS), np.float32)
    for q in range(QUARTERS):
        for a in range(2):
            for t in range(TOK):
                row = q * 2 * TOK + a * TOK + t
                fold[q, row, a * 8 + t] = 1
                last[q, a * 8 + t, row] = 1
                for w in range(8):
                    unfold[q, a * GROUP + w * TOK + t, w * ROWS + row] = 1
    back = np.transpose(unfold, (0, 2, 1))
    return [jnp.asarray(v, BF16) for v in (fold, unfold, back, last)]


def dot(a, b):
    return lax.dot_general(a, b, (((1,), (0,)), ((), ())), preferred_element_type=F32)


def dot_t(a, b):
    return lax.dot_general(a, b, (((1,), (1,)), ((), ())), preferred_element_type=F32)


def t_dot(a, b):
    return lax.dot_general(a, b, (((0,), (0,)), ((), ())), preferred_element_type=F32)


def kernel(
    zs, act_ref, cot_ref, wg_hbm, wu_hbm, wd_hbm, fold_ref, unfold_hbm, back_hbm, last_ref,
    out_ref, gin_ref, gg_ref, gu_ref, gd_ref,
    wg, wu, wd, unfold, back, stage16, g_buf, acts, cots,
    pa, pb, ra, rb, qa, qb, a1, b1, sa, sb, a2, b2, ha, hb, hd,
    own_sum, xs, xr_buf, rbuf, rw, fsend, frecv,
    local_sem, send_sem, recv_sem,
):
    dp, tn = lax.axis_index("dp"), lax.axis_index("tensor")
    z, xh = dp // 2, dp % 2
    xl, y, c = tn // 8, (tn // 2) % 4, tn % 2
    xo, co = 1 - xl, 1 - c

    def z_dev(d):
        return (((z + (d + zs)) % zs) * 2 + xh, tn)

    def t_dev(x_, y_, c_):
        return (dp, (x_ * 4 + y_) * 2 + c_)

    def y_at(d):
        return (y + d) % 4

    def x2_at(d):
        return (((z + (d + zs)) % zs) * 2 + (1 - xh), tn)

    x2_dev = x2_at(0)
    x1_dev = t_dev(xo, y, c)
    c_dev = t_dev(xl, y, co)

    loads = []
    for i, (s, d) in enumerate(
        ((wg_hbm, wg), (wu_hbm, wu), (wd_hbm, wd), (unfold_hbm, unfold), (back_hbm, back))
    ):
        cp = pltpu.make_async_copy(s, d, local_sem.at[i])
        cp.start()
        loads.append(cp)

    barrier = pltpu.get_barrier_semaphore()
    peers = [z_dev(d) for d in (8, -8, 4, -4, 2, -2, 1, -1)]
    peers += [x2_dev, x2_at(1), x2_at(-1), x1_dev, c_dev] + [t_dev(xl, y_at(d), c) for d in (1, 2, 3)]
    for peer in peers:
        pl.semaphore_signal(barrier, inc=1, device_id=peer, device_id_type=MESH)

    sent = []

    def send(src, dst, dev):
        i = len(sent)
        cp = pltpu.make_async_remote_copy(
            src_ref=src, dst_ref=dst, send_sem=send_sem.at[i], recv_sem=recv_sem.at[i],
            device_id=dev, device_id_type=MESH,
        )
        cp.start()
        sent.append(cp)
        return cp

    stage16[...] = jnp.zeros_like(stage16)
    stage16[0:TOK] = act_ref[...].astype(F32)
    stage16[8 : 8 + TOK] = cot_ref[...].astype(F32)
    raw = stage16[...].astype(BF16)
    block = jnp.zeros((ROWS, 128), F32)
    for q in range(QUARTERS):
        block += dot(fold_ref[q], raw[:, q * 128 : (q + 1) * 128])
    g_buf[0, 0, 0] = block.astype(BF16)

    pl.semaphore_wait(barrier, len(peers))

    own = g_buf.at[0, F0, 0]
    far = {}
    far[M8] = send(own, g_buf.at[0, M8, 0], z_dev(8))
    far[P8] = send(own, g_buf.at[0, P8, 0], z_dev(-8))
    far[M4] = send(own, g_buf.at[0, M4, 0], z_dev(4))
    far[P4] = send(own, g_buf.at[0, P4, 0], z_dev(-4))
    near, across = {}, {}

    def spread(f):
        block = g_buf.at[0, f, 0]
        near[f, 1] = send(block, g_buf.at[0, f, 1], z_dev(-1))
        near[f, 2] = send(block, g_buf.at[0, f, 2], z_dev(1))
        if f in ABOVE:
            near[f, 3] = send(block, g_buf.at[0, f, 3], z_dev(-2))
        for slot, source in BELOW.items():
            if source == f:
                near[slot, 3] = send(block, g_buf.at[0, slot, 3], z_dev(2))

    def cross(f):
        for w in (1, 2, 3):
            near[f, w].wait_recv()
        across[f] = send(g_buf.at[0, f], g_buf.at[1, f], x2_dev)

    def order(x, g):
        blocks = g_buf[x, 2 * g : 2 * g + 2].reshape(BLOCKS * ROWS, 128)
        for q in range(QUARTERS):
            rows = dot(unfold[q], blocks).astype(BF16)
            lanes = slice(q * 128, (q + 1) * 128)
            acts[x, g, :, lanes] = rows[:GROUP]
            cots[x, g, :, lanes] = rows[GROUP:]

    def order_other(g):
        across[2 * g].wait_recv()
        if g == 3:
            for cp in last:
                cp.wait_recv()
        else:
            across[2 * g + 1].wait_recv()
        order(1, g)

    spread(F0)
    far[P4].wait_recv()
    spread(P4)
    far[M4].wait_recv()
    spread(M4)
    far[M8].wait_recv()
    far[P8].wait_recv()
    odd = z % 2
    far[F16] = send(g_buf.at[0, M8 - odd, 0], g_buf.at[0, F16, 0], z_dev(8 + (zs - 16) * odd))
    far[M12] = send(g_buf.at[0, M8, 0], g_buf.at[0, M12, 0], z_dev(4))
    far[P12] = send(g_buf.at[0, P8, 0], g_buf.at[0, P12, 0], z_dev(-4))
    spread(P8)
    spread(M8)
    cross(F0)
    cross(P4)
    cross(M4)
    for cp in loads:
        cp.wait()
    order(0, 0)
    cross(P8)
    cross(M8)
    far[M12].wait_recv()
    spread(M12)
    far[P12].wait_recv()
    spread(P12)
    order(0, 1)
    far[F16].wait_recv()
    spread(F16)
    last = [
        send(g_buf.at[0, F16, 0], g_buf.at[1, F16, 0], x2_dev),
        send(g_buf.at[0, F16, 0], g_buf.at[1, F16, 1], x2_at(-1)),
        send(g_buf.at[0, F16, 0], g_buf.at[1, F16, 2], x2_at(1)),
    ]
    cross(P12)
    cross(M12)
    near[F16, 3].wait_recv()
    last.append(send(g_buf.at[0, F16, 3], g_buf.at[1, F16, 3], x2_dev))
    order(0, 2)
    order_other(0)
    near[F16, 1].wait_recv()
    near[F16, 2].wait_recv()
    order(0, 3)

    pair = {}

    def partial_sums(x):
        a_rows = acts[x].reshape(4 * GROUP, 512)
        c_rows = cots[x].reshape(4 * GROUP, 512)
        for j, (rows, weight) in enumerate(((a_rows, wg), (a_rows, wu), (c_rows, wd))):
            part = slice(j * GROUP, (j + 1) * GROUP)
            low = dot_t(rows, weight[0:256])
            high = dot_t(rows, weight[256:448])
            for f in range(4):
                r = slice(f * GROUP, (f + 1) * GROUP)
                pa[0, f, x, part] = low[r, 0:128]
                pb[0, x, f, part] = low[r, 128:256]
                pa[1, f, x, part] = high[r, 0:128]
                pb[1, x, f, part, 0:64] = high[r, 128:192]
                pb[1, x, f, part, 64:128] = jnp.zeros((GROUP, 64), F32)
        pair[x, 0] = send(pa.at[co, :, x], ra.at[:, x], c_dev)
        pair[x, 1] = send(pb.at[co, x], rb.at[x], c_dev)

    first_a = []

    def along_y(x):
        pair[x, 0].wait_recv()
        qa[:, x] = pa[c, :, x] + ra[:, x]
        for d in (2, 1, 3):
            dev = t_dev(xl, y_at(d), c)
            first_a.append(send(qa.at[y_at(d), x], a1.at[d - 1, x], dev))

    partial_sums(0)
    order_other(1)
    along_y(0)
    order_other(2)
    order_other(3)
    partial_sums(1)

    pair[0, 1].wait_recv()
    pair[1, 1].wait_recv()
    first_b, second_b = {}, []
    for d in (2, 1, 3, 0):
        r = y_at(d)
        qb[xo, r] = pb[c, xo, r] + rb[xo, r]
        first_b[d] = send(qb.at[xo, r], b1.at[r], x1_dev)
    along_y(1)
    qb[xl] = pb[c, xl] + rb[xl]
    for d in (2, 1, 3):
        r = y_at(d)
        first_b[d].wait_recv()
        sb[r] = qb[xl, r] + b1[r]
        second_b.append(send(sb.at[r], b2.at[d - 1], t_dev(xl, r, c)))
    for cp in first_a:
        cp.wait_recv()
    sa[xo] = qa[y, xo] + a1[0, xo] + a1[1, xo] + a1[2, xo]
    second_a = send(sa.at[xo], a2, x1_dev)
    sa[xl] = qa[y, xl] + a1[0, xl] + a1[1, xl] + a1[2, xl]
    first_b[0].wait_recv()
    sb[y] = qb[xl, y] + b1[y]

    def finish(sums):
        gate, up, grad = sums[0:GROUP], sums[GROUP : 2 * GROUP], sums[2 * GROUP : 3 * GROUP]
        s = jax.nn.sigmoid(gate)
        silu = gate * s
        hidden = (silu * up).astype(BF16)
        d_gate = (grad * up * s * (1.0 + gate * (1.0 - s))).astype(BF16)
        d_up = (grad * silu).astype(BF16)
        return jnp.concatenate([hidden, d_gate, d_up], axis=0)

    y_peers = [(d, t_dev(xl, y_at(d), c)) for d in (2, 1, 3)]
    cores = []
    second_a.wait_recv()
    ha[c, y, xl] = finish(sa[xl] + a2[...])
    near_a = send(ha.at[c, y, xl], ha.at[c, y, xl], x1_dev)
    for cp in second_b:
        cp.wait_recv()
    hb[c, xl, y] = finish(sb[y] + b2[0] + b2[1] + b2[2])
    near_b = [send(hb.at[c, xl, y], hb.at[c, xl, y], dev) for d, dev in y_peers]
    near_a.wait_recv()
    wide_a = [send(ha.at[c, y], ha.at[c, y], dev) for d, dev in y_peers]
    cores.append(send(ha.at[c, y], ha.at[c, y], c_dev))
    for cp in near_b:
        cp.wait_recv()
    wide_b = send(hb.at[c, xl], hb.at[c, xl], x1_dev)
    cores.append(send(hb.at[c, xl], hb.at[c, xl], c_dev))
    for (d, dev), cp in zip(y_peers, wide_a):
        cp.wait_recv()
        cores.append(send(ha.at[c, y_at(4 - d)], ha.at[c, y_at(4 - d)], c_dev))
    wide_b.wait_recv()
    cores.append(send(hb.at[c, xo], hb.at[c, xo], c_dev))
    for cp in cores:
        cp.wait_recv()

    for j in range(3):
        part = slice(j * GROUP, (j + 1) * GROUP)
        for half in range(2):
            for x in range(2):
                for f in range(4):
                    hd[j, x, f, :, half * 256 : half * 256 + 128] = ha[half, f, x, part]
                    hd[j, x, f, :, half * 256 + 128 : half * 256 + 256] = hb[half, x, f, part]

    def hidden_sums(x):
        h, dg, du = [hd[j, x].reshape(4 * GROUP, 512)[:, :448] for j in range(3)]
        return dot(h, wd[...]), dot(dg, wg[...]) + dot(du, wu[...])

    over = {}

    def give(g):
        over[g] = send(xs.at[g], xr_buf.at[g], x2_dev)

    fwd, bwd = hidden_sums(1)
    for g in range(4):
        r = slice(g * GROUP, (g + 1) * GROUP)
        xs[g, 0:GROUP] = fwd[r].astype(BF16)
        xs[g, GROUP : 2 * GROUP] = bwd[r].astype(BF16)
    give(3)
    fwd, bwd = hidden_sums(0)
    give(2)
    for g in range(4):
        r = slice(g * GROUP, (g + 1) * GROUP)
        own_sum[g, 0:GROUP] = fwd[r]
        own_sum[g, GROUP : 2 * GROUP] = bwd[r]

    part_in = {}

    def collect(g):
        over[g].wait_recv()
        both = (own_sum[g] + xr_buf[g].astype(F32)).astype(BF16)
        rows = jnp.zeros((BLOCKS * ROWS, 128), F32)
        for q in range(QUARTERS):
            rows += dot(back[q], both[:, q * 128 : (q + 1) * 128])
        rows = rows.astype(BF16)
        for i in range(BLOCKS):
            rbuf[2 * g + i // 4, i % 4] = rows[i * ROWS : (i + 1) * ROWS]
        for f in (2 * g + 1, 2 * g):
            part_in[f, 0] = send(rbuf.at[f, 1], rw.at[f, 0], z_dev(1))
            part_in[f, 1] = send(rbuf.at[f, 2], rw.at[f, 1], z_dev(-1))
            if f in ABOVE:
                part_in[f, 2] = send(rbuf.at[f, 3], rw.at[f, 2], z_dev(2))
            else:
                part_in[BELOW[f], 3] = send(rbuf.at[f, 3], rw.at[BELOW[f], 3], z_dev(-2))

    def near_sum(f):
        total = rbuf[f, 0].astype(F32)
        for i in range(4):
            if (f, i) in part_in:
                part_in[f, i].wait_recv()
                total += rw[f, i].astype(F32)
        return total

    onward = {}

    def pass_on(i, f, dev, *others):
        total = near_sum(f)
        for o in others:
            onward[o].wait_recv()
            total += frecv[o].astype(F32)
        fsend[i] = total.astype(BF16)
        onward[i] = send(fsend.at[i], frecv.at[i], dev)

    def weight_grad(j, tokens, ref):
        d = hd[j].reshape(8 * GROUP, 512)
        rows = tokens[...].reshape(8 * GROUP, 512)
        ref[0:256] = t_dot(d[:, 0:256], rows).astype(BF16)
        ref[256:448] = t_dot(d[:, 256:448], rows).astype(BF16)

    weight_grad(1, acts, gg_ref)
    collect(3)
    give(1)
    give(0)
    collect(2)
    pass_on(0, F16, z_dev(8))
    collect(1)
    pass_on(2, M12, z_dev(-4))
    pass_on(1, P12, z_dev(4))
    weight_grad(2, acts, gu_ref)
    collect(0)
    pass_on(4, M8, z_dev(-8), 2)
    pass_on(3, P8, z_dev(8), 1, 0)
    pass_on(5, P4, z_dev(4))
    pass_on(6, M4, z_dev(-4))
    weight_grad(0, cots, gd_ref)

    total = near_sum(F0)
    for o in (5, 6, 4, 3):
        onward[o].wait_recv()
        total += frecv[o].astype(F32)
    total = total.astype(BF16)
    for q in range(QUARTERS):
        stage16[:, q * 128 : (q + 1) * 128] = dot(last_ref[q], total)
    out_ref[...] = stage16[0:TOK].astype(BF16)
    gin_ref[...] = stage16[8 : 8 + TOK].astype(BF16)
    for cp in sent:
        cp.wait_send()


def hand_over(*refs):
    sem = refs[-1]
    copies = [pltpu.make_async_copy(refs[i], refs[5 + i], sem.at[i]) for i in range(5)]
    for cp in copies:
        cp.start()
    for cp in copies:
        cp.wait()


def on_device(zs, activations, cotangent, w_gate, w_up, w_down):
    tokens, features = activations.shape
    hidden = w_gate.shape[0]
    fold, unfold, back, last = selections()
    vmem = pl.BlockSpec(memory_space=pltpu.VMEM)
    anywhere = pl.BlockSpec(memory_space=pl.ANY)
    weight = (hidden, features)
    row3 = 3 * GROUP
    scratch = [
        pltpu.VMEM(weight, BF16), pltpu.VMEM(weight, BF16), pltpu.VMEM(weight, BF16),
        pltpu.VMEM(unfold.shape, BF16), pltpu.VMEM(back.shape, BF16),
        pltpu.VMEM((16, features), F32),
        pltpu.VMEM((2, 8, 4, ROWS, 128), BF16),
        pltpu.VMEM((2, 4, GROUP, features), BF16), pltpu.VMEM((2, 4, GROUP, features), BF16),
        pltpu.VMEM((2, 4, 2, row3, 128), F32), pltpu.VMEM((2, 2, 4, row3, 128), F32),
        pltpu.VMEM((4, 2, row3, 128), F32), pltpu.VMEM((2, 4, row3, 128), F32),
        pltpu.VMEM((4, 2, row3, 128), F32), pltpu.VMEM((2, 4, row3, 128), F32),
        pltpu.VMEM((3, 2, row3, 128), F32), pltpu.VMEM((4, row3, 128), F32),
        pltpu.VMEM((2, row3, 128), F32), pltpu.VMEM((4, row3, 128), F32),
        pltpu.VMEM((row3, 128), F32), pltpu.VMEM((3, row3, 128), F32),
        pltpu.VMEM((2, 4, 2, row3, 128), BF16), pltpu.VMEM((2, 2, 4, row3, 128), BF16),
        pltpu.VMEM((3, 2, 4, GROUP, 512), BF16),
        pltpu.VMEM((4, 2 * GROUP, features), F32),
        pltpu.VMEM((4, 2 * GROUP, features), BF16), pltpu.VMEM((4, 2 * GROUP, features), BF16),
        pltpu.VMEM((8, 4, ROWS, 128), BF16), pltpu.VMEM((8, 4, ROWS, 128), BF16),
        pltpu.VMEM((7, ROWS, 128), BF16), pltpu.VMEM((7, ROWS, 128), BF16),
        pltpu.SemaphoreType.DMA((5,)),
        pltpu.SemaphoreType.DMA((N_COPIES,)), pltpu.SemaphoreType.DMA((N_COPIES,)),
    ]
    block = jax.ShapeDtypeStruct((tokens, features), BF16)
    grad = jax.ShapeDtypeStruct(weight, BF16)
    results = pl.pallas_call(
        functools.partial(kernel, zs),
        out_shape=(block, block, grad, grad, grad),
        in_specs=[vmem, vmem, anywhere, anywhere, anywhere, vmem, anywhere, anywhere, vmem],
        out_specs=(vmem,) * 5,
        scratch_shapes=scratch,
        compiler_params=pltpu.CompilerParams(
            collective_id=0, has_side_effects=True, vmem_limit_bytes=56 * 2**20
        ),
        cost_estimate=pl.CostEstimate(
            flops=18 * 384 * hidden * features, bytes_accessed=12 * hidden * features,
            transcendentals=0,
        ),
        name="ffn",
    )(activations, cotangent, w_gate, w_up, w_down, fold, unfold, back, last)
    return pl.pallas_call(
        hand_over,
        out_shape=(block, block, grad, grad, grad),
        in_specs=[vmem] * 5,
        out_specs=(anywhere,) * 5,
        scratch_shapes=[pltpu.SemaphoreType.DMA((5,))],
        name="hand_over",
    )(*results)


def solution(mesh):
    spec = P("dp", "tensor")
    return jax.shard_map(
        functools.partial(on_device, mesh.shape["dp"] // 2),
        mesh=mesh,
        in_specs=(spec,) * 5,
        out_specs=(spec,) * 5,
        check_vma=False,
    )
```

```python
import functools

import jax
import jax.numpy as jnp
import numpy as np
from jax import lax
from jax.experimental import pallas as pl
from jax.experimental.pallas import tpu as pltpu
from jax.sharding import PartitionSpec as P

MESH = pl.DeviceIdType.MESH
F32 = jnp.float32
BF16 = jnp.bfloat16

NEAR = (0, 1, -1, 2)
FAR = (0, 4, -4, 8, -8, 12, -12, 16)
F0, P4, M4, P8, M8, P12, M12, F16 = range(8)
ABOVE = (F0, P4, P8, P12)
BELOW = {M4: F0, M8: M4, M12: M8, F16: M12}
TOK = 6
QUARTERS = 4
ROWS = 2 * TOK * QUARTERS
BLOCKS = 8
GROUP = TOK * BLOCKS
N_COPIES = 160


def selections():
    fold = np.zeros((QUARTERS, ROWS, 16), np.float32)
    unfold = np.zeros((QUARTERS, 2 * GROUP, 8 * ROWS), np.float32)
    last = np.zeros((QUARTERS, 16, ROWS), np.float32)
    for q in range(QUARTERS):
        for a in range(2):
            for t in range(TOK):
                row = q * 2 * TOK + a * TOK + t
                fold[q, row, a * 8 + t] = 1
                last[q, a * 8 + t, row] = 1
                for w in range(8):
                    unfold[q, a * GROUP + w * TOK + t, w * ROWS + row] = 1
    back = np.transpose(unfold, (0, 2, 1))
    return [jnp.asarray(v, BF16) for v in (fold, unfold, back, last)]


def dot(a, b):
    return lax.dot_general(a, b, (((1,), (0,)), ((), ())), preferred_element_type=F32)


def dot_t(a, b):
    return lax.dot_general(a, b, (((1,), (1,)), ((), ())), preferred_element_type=F32)


def t_dot(a, b):
    return lax.dot_general(a, b, (((0,), (0,)), ((), ())), preferred_element_type=F32)


def kernel(
    zs, act_hbm, cot_hbm, wg_hbm, wu_hbm, wd_hbm, fold_hbm, unfold_hbm, back_hbm, last_hbm,
    out_ref, gin_ref, gg_hbm, gu_hbm, gd_hbm,
    act_ref, cot_ref, fold_ref, last_ref, grads,
    wg, wu, wd, unfold, back, stage16, g_buf, acts, cots,
    pa, pb, ra, rb, qa, qb, a1, b1, sa, sb, a2, b2, ha, hb, hd,
    own_sum, xs, xr_buf, rbuf, rw, fsend, frecv,
    local_sem, send_sem, recv_sem,
):
    dp, tn = lax.axis_index("dp"), lax.axis_index("tensor")
    z, xh = dp // 2, dp % 2
    xl, y, c = tn // 8, (tn // 2) % 4, tn % 2
    xo, co = 1 - xl, 1 - c

    def z_dev(d):
        return (((z + (d + zs)) % zs) * 2 + xh, tn)

    def t_dev(x_, y_, c_):
        return (dp, (x_ * 4 + y_) * 2 + c_)

    def y_at(d):
        return (y + d) % 4

    def x2_at(d):
        return (((z + (d + zs)) % zs) * 2 + (1 - xh), tn)

    x2_dev = x2_at(0)
    x1_dev = t_dev(xo, y, c)
    c_dev = t_dev(xl, y, co)

    barrier = pltpu.get_barrier_semaphore()
    peers = [z_dev(d) for d in (8, -8, 4, -4, 2, -2, 1, -1)]
    peers += [x2_dev, x2_at(1), x2_at(-1), x1_dev, c_dev] + [t_dev(xl, y_at(d), c) for d in (1, 2, 3)]
    for peer in peers:
        pl.semaphore_signal(barrier, inc=1, device_id=peer, device_id_type=MESH)

    loads = []
    for i, (s, d) in enumerate(
        ((act_hbm, act_ref), (cot_hbm, cot_ref), (fold_hbm, fold_ref), (wg_hbm, wg), (wu_hbm, wu), (wd_hbm, wd),
         (unfold_hbm, unfold), (back_hbm, back), (last_hbm, last_ref))
    ):
        cp = pltpu.make_async_copy(s, d, local_sem.at[i])
        cp.start()
        loads.append(cp)

    sent = []

    def send(src, dst, dev):
        i = len(sent)
        cp = pltpu.make_async_remote_copy(
            src_ref=src, dst_ref=dst, send_sem=send_sem.at[i], recv_sem=recv_sem.at[i],
            device_id=dev, device_id_type=MESH,
        )
        cp.start()
        sent.append(cp)
        return cp

    stage16[...] = jnp.zeros_like(stage16)
    for cp in loads[:3]:
        cp.wait()
    stage16[0:TOK] = act_ref[...].astype(F32)
    stage16[8 : 8 + TOK] = cot_ref[...].astype(F32)
    raw = stage16[...].astype(BF16)
    block = jnp.zeros((ROWS, 128), F32)
    for q in range(QUARTERS):
        block += dot(fold_ref[q], raw[:, q * 128 : (q + 1) * 128])
    g_buf[0, 0, 0] = block.astype(BF16)

    pl.semaphore_wait(barrier, len(peers))

    own = g_buf.at[0, F0, 0]
    far = {}
    far[M8] = send(own, g_buf.at[0, M8, 0], z_dev(8))
    far[P8] = send(own, g_buf.at[0, P8, 0], z_dev(-8))
    far[M4] = send(own, g_buf.at[0, M4, 0], z_dev(4))
    far[P4] = send(own, g_buf.at[0, P4, 0], z_dev(-4))
    near, across = {}, {}

    def spread(f):
        block = g_buf.at[0, f, 0]
        near[f, 1] = send(block, g_buf.at[0, f, 1], z_dev(-1))
        near[f, 2] = send(block, g_buf.at[0, f, 2], z_dev(1))
        if f in ABOVE:
            near[f, 3] = send(block, g_buf.at[0, f, 3], z_dev(-2))
        for slot, source in BELOW.items():
            if source == f:
                near[slot, 3] = send(block, g_buf.at[0, slot, 3], z_dev(2))

    def cross(f):
        for w in (1, 2, 3):
            near[f, w].wait_recv()
        across[f] = send(g_buf.at[0, f], g_buf.at[1, f], x2_dev)

    def order(x, g):
        blocks = g_buf[x, 2 * g : 2 * g + 2].reshape(BLOCKS * ROWS, 128)
        for q in range(QUARTERS):
            rows = dot(unfold[q], blocks).astype(BF16)
            lanes = slice(q * 128, (q + 1) * 128)
            acts[x, g, :, lanes] = rows[:GROUP]
            cots[x, g, :, lanes] = rows[GROUP:]

    def order_other(g):
        across[2 * g].wait_recv()
        if g == 3:
            for cp in last:
                cp.wait_recv()
        else:
            across[2 * g + 1].wait_recv()
        order(1, g)

    spread(F0)
    far[P4].wait_recv()
    spread(P4)
    far[M4].wait_recv()
    spread(M4)
    far[M8].wait_recv()
    far[P8].wait_recv()
    odd = z % 2
    far[F16] = send(g_buf.at[0, M8 - odd, 0], g_buf.at[0, F16, 0], z_dev(8 + (zs - 16) * odd))
    far[M12] = send(g_buf.at[0, M8, 0], g_buf.at[0, M12, 0], z_dev(4))
    far[P12] = send(g_buf.at[0, P8, 0], g_buf.at[0, P12, 0], z_dev(-4))
    spread(P8)
    spread(M8)
    cross(F0)
    cross(P4)
    cross(M4)
    for cp in loads[3:]:
        cp.wait()
    order(0, 0)
    cross(P8)
    cross(M8)
    far[M12].wait_recv()
    spread(M12)
    far[P12].wait_recv()
    spread(P12)
    order(0, 1)
    far[F16].wait_recv()
    spread(F16)
    last = [
        send(g_buf.at[0, F16, 0], g_buf.at[1, F16, 0], x2_dev),
        send(g_buf.at[0, F16, 0], g_buf.at[1, F16, 1], x2_at(-1)),
        send(g_buf.at[0, F16, 0], g_buf.at[1, F16, 2], x2_at(1)),
    ]
    cross(P12)
    cross(M12)
    near[F16, 3].wait_recv()
    last.append(send(g_buf.at[0, F16, 3], g_buf.at[1, F16, 3], x2_dev))
    order(0, 2)
    order_other(0)
    near[F16, 1].wait_recv()
    near[F16, 2].wait_recv()
    order(0, 3)

    pair = {}

    def partial_sums(x):
        a_rows = acts[x].reshape(4 * GROUP, 512)
        c_rows = cots[x].reshape(4 * GROUP, 512)
        for j, (rows, weight) in enumerate(((a_rows, wg), (a_rows, wu), (c_rows, wd))):
            part = slice(j * GROUP, (j + 1) * GROUP)
            low = dot_t(rows, weight[0:256])
            high = dot_t(rows, weight[256:448])
            for f in range(4):
                r = slice(f * GROUP, (f + 1) * GROUP)
                pa[0, f, x, part] = low[r, 0:128]
                pb[0, x, f, part] = low[r, 128:256]
                pa[1, f, x, part] = high[r, 0:128]
                pb[1, x, f, part, 0:64] = high[r, 128:192]
                pb[1, x, f, part, 64:128] = jnp.zeros((GROUP, 64), F32)
        pair[x, 0] = send(pa.at[co, :, x], ra.at[:, x], c_dev)
        pair[x, 1] = send(pb.at[co, x], rb.at[x], c_dev)

    first_a = []

    def along_y(x):
        pair[x, 0].wait_recv()
        qa[:, x] = pa[c, :, x] + ra[:, x]
        for d in (2, 1, 3):
            dev = t_dev(xl, y_at(d), c)
            first_a.append(send(qa.at[y_at(d), x], a1.at[d - 1, x], dev))

    partial_sums(0)
    order_other(1)
    along_y(0)
    order_other(2)
    order_other(3)
    partial_sums(1)

    pair[0, 1].wait_recv()
    pair[1, 1].wait_recv()
    first_b, second_b = {}, []
    for d in (2, 1, 3, 0):
        r = y_at(d)
        qb[xo, r] = pb[c, xo, r] + rb[xo, r]
        first_b[d] = send(qb.at[xo, r], b1.at[r], x1_dev)
    along_y(1)
    qb[xl] = pb[c, xl] + rb[xl]
    for d in (2, 1, 3):
        r = y_at(d)
        first_b[d].wait_recv()
        sb[r] = qb[xl, r] + b1[r]
        second_b.append(send(sb.at[r], b2.at[d - 1], t_dev(xl, r, c)))
    for cp in first_a:
        cp.wait_recv()
    sa[xo] = qa[y, xo] + a1[0, xo] + a1[1, xo] + a1[2, xo]
    second_a = send(sa.at[xo], a2, x1_dev)
    sa[xl] = qa[y, xl] + a1[0, xl] + a1[1, xl] + a1[2, xl]
    first_b[0].wait_recv()
    sb[y] = qb[xl, y] + b1[y]

    def finish(sums):
        gate, up, grad = sums[0:GROUP], sums[GROUP : 2 * GROUP], sums[2 * GROUP : 3 * GROUP]
        s = jax.nn.sigmoid(gate)
        silu = gate * s
        hidden = (silu * up).astype(BF16)
        d_gate = (grad * up * s * (1.0 + gate * (1.0 - s))).astype(BF16)
        d_up = (grad * silu).astype(BF16)
        return jnp.concatenate([hidden, d_gate, d_up], axis=0)

    y_peers = [(d, t_dev(xl, y_at(d), c)) for d in (2, 1, 3)]
    cores = []
    second_a.wait_recv()
    ha[c, y, xl] = finish(sa[xl] + a2[...])
    near_a = send(ha.at[c, y, xl], ha.at[c, y, xl], x1_dev)
    for cp in second_b:
        cp.wait_recv()
    hb[c, xl, y] = finish(sb[y] + b2[0] + b2[1] + b2[2])
    near_b = [send(hb.at[c, xl, y], hb.at[c, xl, y], dev) for d, dev in y_peers]
    near_a.wait_recv()
    wide_a = [send(ha.at[c, y], ha.at[c, y], dev) for d, dev in y_peers]
    cores.append(send(ha.at[c, y], ha.at[c, y], c_dev))
    for cp in near_b:
        cp.wait_recv()
    wide_b = send(hb.at[c, xl], hb.at[c, xl], x1_dev)
    cores.append(send(hb.at[c, xl], hb.at[c, xl], c_dev))
    for (d, dev), cp in zip(y_peers, wide_a):
        cp.wait_recv()
        cores.append(send(ha.at[c, y_at(4 - d)], ha.at[c, y_at(4 - d)], c_dev))
    wide_b.wait_recv()
    cores.append(send(hb.at[c, xo], hb.at[c, xo], c_dev))
    for cp in cores:
        cp.wait_recv()

    for j in range(3):
        part = slice(j * GROUP, (j + 1) * GROUP)
        for half in range(2):
            for x in range(2):
                for f in range(4):
                    hd[j, x, f, :, half * 256 : half * 256 + 128] = ha[half, f, x, part]
                    hd[j, x, f, :, half * 256 + 128 : half * 256 + 256] = hb[half, x, f, part]

    def hidden_sums(x):
        h, dg, du = [hd[j, x].reshape(4 * GROUP, 512)[:, :448] for j in range(3)]
        return dot(h, wd[...]), dot(dg, wg[...]) + dot(du, wu[...])

    over = {}

    def give(g):
        over[g] = send(xs.at[g], xr_buf.at[g], x2_dev)

    fwd, bwd = hidden_sums(1)
    for g in range(4):
        r = slice(g * GROUP, (g + 1) * GROUP)
        xs[g, 0:GROUP] = fwd[r].astype(BF16)
        xs[g, GROUP : 2 * GROUP] = bwd[r].astype(BF16)
    give(3)
    fwd, bwd = hidden_sums(0)
    give(2)
    for g in range(4):
        r = slice(g * GROUP, (g + 1) * GROUP)
        own_sum[g, 0:GROUP] = fwd[r]
        own_sum[g, GROUP : 2 * GROUP] = bwd[r]

    part_in = {}

    def collect(g):
        over[g].wait_recv()
        both = (own_sum[g] + xr_buf[g].astype(F32)).astype(BF16)
        rows = jnp.zeros((BLOCKS * ROWS, 128), F32)
        for q in range(QUARTERS):
            rows += dot(back[q], both[:, q * 128 : (q + 1) * 128])
        rows = rows.astype(BF16)
        for i in range(BLOCKS):
            rbuf[2 * g + i // 4, i % 4] = rows[i * ROWS : (i + 1) * ROWS]
        for f in (2 * g + 1, 2 * g):
            part_in[f, 0] = send(rbuf.at[f, 1], rw.at[f, 0], z_dev(1))
            part_in[f, 1] = send(rbuf.at[f, 2], rw.at[f, 1], z_dev(-1))
            if f in ABOVE:
                part_in[f, 2] = send(rbuf.at[f, 3], rw.at[f, 2], z_dev(2))
            else:
                part_in[BELOW[f], 3] = send(rbuf.at[f, 3], rw.at[BELOW[f], 3], z_dev(-2))

    def near_sum(f):
        total = rbuf[f, 0].astype(F32)
        for i in range(4):
            if (f, i) in part_in:
                part_in[f, i].wait_recv()
                total += rw[f, i].astype(F32)
        return total

    onward = {}

    def pass_on(i, f, dev, *others):
        total = near_sum(f)
        for o in others:
            onward[o].wait_recv()
            total += frecv[o].astype(F32)
        fsend[i] = total.astype(BF16)
        onward[i] = send(fsend.at[i], frecv.at[i], dev)

    stores = []

    def weight_grad(j, tokens, result):
        ref = grads.at[j]
        d = hd[j].reshape(8 * GROUP, 512)
        rows = tokens[...].reshape(8 * GROUP, 512)
        ref[0:256] = t_dot(d[:, 0:256], rows).astype(BF16)
        ref[256:448] = t_dot(d[:, 256:448], rows).astype(BF16)
        stores.append(pltpu.make_async_copy(ref, result, local_sem.at[9 + j]))
        stores[-1].start()

    weight_grad(1, acts, gg_hbm)
    collect(3)
    give(1)
    give(0)
    collect(2)
    pass_on(0, F16, z_dev(8))
    collect(1)
    pass_on(2, M12, z_dev(-4))
    pass_on(1, P12, z_dev(4))
    weight_grad(2, acts, gu_hbm)
    collect(0)
    pass_on(4, M8, z_dev(-8), 2)
    pass_on(3, P8, z_dev(8), 1, 0)
    pass_on(5, P4, z_dev(4))
    pass_on(6, M4, z_dev(-4))
    weight_grad(0, cots, gd_hbm)

    total = near_sum(F0)
    for o in (5, 6, 4, 3):
        onward[o].wait_recv()
        total += frecv[o].astype(F32)
    total = total.astype(BF16)
    for q in range(QUARTERS):
        stage16[:, q * 128 : (q + 1) * 128] = dot(last_ref[q], total)
    out_ref[...] = stage16[0:TOK].astype(BF16)
    gin_ref[...] = stage16[8 : 8 + TOK].astype(BF16)
    for cp in sent:
        cp.wait_send()
    for cp in stores:
        cp.wait()


def hand_over(*refs):
    sem = refs[-1]
    loads = [pltpu.make_async_copy(refs[i], refs[10 + i], sem.at[i]) for i in range(5)]
    stores = [pltpu.make_async_copy(refs[10 + i], refs[5 + i], sem.at[5 + i]) for i in range(5)]
    turns = (2, 3, 4, 0, 1)
    for i in turns:
        loads[i].start()
    for i in turns:
        loads[i].wait()
        stores[i].start()
    for i in turns:
        stores[i].wait()


def on_device(zs, activations, cotangent, w_gate, w_up, w_down):
    tokens, features = activations.shape
    hidden = w_gate.shape[0]
    fold, unfold, back, last = selections()
    vmem = pl.BlockSpec(memory_space=pltpu.VMEM)
    anywhere = pl.BlockSpec(memory_space=pl.ANY)
    weight = (hidden, features)
    row3 = 3 * GROUP
    scratch = [
        pltpu.VMEM((tokens, features), BF16), pltpu.VMEM((tokens, features), BF16),
        pltpu.VMEM(fold.shape, BF16), pltpu.VMEM(last.shape, BF16),
        pltpu.VMEM((3,) + weight, BF16),
        pltpu.VMEM(weight, BF16), pltpu.VMEM(weight, BF16), pltpu.VMEM(weight, BF16),
        pltpu.VMEM(unfold.shape, BF16), pltpu.VMEM(back.shape, BF16),
        pltpu.VMEM((16, features), F32),
        pltpu.VMEM((2, 8, 4, ROWS, 128), BF16),
        pltpu.VMEM((2, 4, GROUP, features), BF16), pltpu.VMEM((2, 4, GROUP, features), BF16),
        pltpu.VMEM((2, 4, 2, row3, 128), F32), pltpu.VMEM((2, 2, 4, row3, 128), F32),
        pltpu.VMEM((4, 2, row3, 128), F32), pltpu.VMEM((2, 4, row3, 128), F32),
        pltpu.VMEM((4, 2, row3, 128), F32), pltpu.VMEM((2, 4, row3, 128), F32),
        pltpu.VMEM((3, 2, row3, 128), F32), pltpu.VMEM((4, row3, 128), F32),
        pltpu.VMEM((2, row3, 128), F32), pltpu.VMEM((4, row3, 128), F32),
        pltpu.VMEM((row3, 128), F32), pltpu.VMEM((3, row3, 128), F32),
        pltpu.VMEM((2, 4, 2, row3, 128), BF16), pltpu.VMEM((2, 2, 4, row3, 128), BF16),
        pltpu.VMEM((3, 2, 4, GROUP, 512), BF16),
        pltpu.VMEM((4, 2 * GROUP, features), F32),
        pltpu.VMEM((4, 2 * GROUP, features), BF16), pltpu.VMEM((4, 2 * GROUP, features), BF16),
        pltpu.VMEM((8, 4, ROWS, 128), BF16), pltpu.VMEM((8, 4, ROWS, 128), BF16),
        pltpu.VMEM((7, ROWS, 128), BF16), pltpu.VMEM((7, ROWS, 128), BF16),
        pltpu.SemaphoreType.DMA((12,)),
        pltpu.SemaphoreType.DMA((N_COPIES,)), pltpu.SemaphoreType.DMA((N_COPIES,)),
    ]
    block = jax.ShapeDtypeStruct((tokens, features), BF16)
    grad = jax.ShapeDtypeStruct(weight, BF16)
    results = pl.pallas_call(
        functools.partial(kernel, zs),
        out_shape=(block, block, grad, grad, grad),
        in_specs=[anywhere] * 9,
        out_specs=(vmem,) * 2 + (anywhere,) * 3,
        scratch_shapes=scratch,
        compiler_params=pltpu.CompilerParams(
            collective_id=0, has_side_effects=True, vmem_limit_bytes=56 * 2**20
        ),
        cost_estimate=pl.CostEstimate(
            flops=18 * 384 * hidden * features, bytes_accessed=12 * hidden * features,
            transcendentals=0,
        ),
        name="ffn",
    )(activations, cotangent, w_gate, w_up, w_down, fold, unfold, back, last)
    return pl.pallas_call(
        hand_over,
        out_shape=(block, block, grad, grad, grad),
        in_specs=[anywhere] * 5,
        out_specs=(anywhere,) * 5,
        scratch_shapes=[pltpu.VMEM(v.shape, BF16) for v in results]
        + [pltpu.SemaphoreType.DMA((10,))],
        name="hand_over",
    )(*results)


def solution(mesh):
    spec = P("dp", "tensor")
    return jax.shard_map(
        functools.partial(on_device, mesh.shape["dp"] // 2),
        mesh=mesh,
        in_specs=(spec,) * 5,
        out_specs=(spec,) * 5,
        check_vma=False,
    )
```

```python
import functools

import jax
import jax.numpy as jnp
import numpy as np
from jax import lax
from jax.experimental import pallas as pl
from jax.experimental.pallas import tpu as pltpu
from jax.sharding import PartitionSpec as P

MESH = pl.DeviceIdType.MESH
F32 = jnp.float32
BF16 = jnp.bfloat16

NEAR = (0, 1, -1, 2)
FAR = (0, 4, -4, 8, -8, 12, -12, 16)
F0, P4, M4, P8, M8, P12, M12, F16 = range(8)
ABOVE = (F0, P4, P8, P12)
BELOW = {M4: F0, M8: M4, M12: M8, F16: M12}
TOK = 6
QUARTERS = 4
ROWS = 2 * TOK * QUARTERS
BLOCKS = 8
GROUP = TOK * BLOCKS
N_COPIES = 160


def selections():
    fold = np.zeros((QUARTERS, ROWS, 16), np.float32)
    unfold = np.zeros((QUARTERS, 2 * GROUP, 8 * ROWS), np.float32)
    last = np.zeros((QUARTERS, 16, ROWS), np.float32)
    for q in range(QUARTERS):
        for a in range(2):
            for t in range(TOK):
                row = q * 2 * TOK + a * TOK + t
                fold[q, row, a * 8 + t] = 1
                last[q, a * 8 + t, row] = 1
                for w in range(8):
                    unfold[q, a * GROUP + w * TOK + t, w * ROWS + row] = 1
    back = np.transpose(unfold, (0, 2, 1))
    return [jnp.asarray(v, BF16) for v in (fold, unfold, back, last)]


def dot(a, b):
    return lax.dot_general(a, b, (((1,), (0,)), ((), ())), preferred_element_type=F32)


def dot_t(a, b):
    return lax.dot_general(a, b, (((1,), (1,)), ((), ())), preferred_element_type=F32)


def t_dot(a, b):
    return lax.dot_general(a, b, (((0,), (0,)), ((), ())), preferred_element_type=F32)


def kernel(
    zs, act_hbm, cot_hbm, wg_hbm, wu_hbm, wd_hbm, fold_hbm, unfold_hbm, back_hbm, last_hbm,
    out_ref, gin_ref, gg_hbm, gu_hbm, gd_hbm,
    act_ref, cot_ref, fold_ref, last_ref, grads,
    wg, wu, wd, unfold, back, stage16, g_buf, acts, cots,
    pa, pb, ra, rb, qa, qb, a1, b1, sa, sb, a2, b2, ha, hb, hd,
    own_sum, xs, xr_buf, rbuf, rw, fsend, frecv,
    local_sem, send_sem, recv_sem,
):
    dp, tn = lax.axis_index("dp"), lax.axis_index("tensor")
    z, xh = dp // 2, dp % 2
    xl, y, c = tn // 8, (tn // 2) % 4, tn % 2
    xo, co = 1 - xl, 1 - c

    def z_dev(d):
        return (((z + (d + zs)) % zs) * 2 + xh, tn)

    def t_dev(x_, y_, c_):
        return (dp, (x_ * 4 + y_) * 2 + c_)

    def y_at(d):
        return (y + d) % 4

    def x2_at(d):
        return (((z + (d + zs)) % zs) * 2 + (1 - xh), tn)

    x2_dev = x2_at(0)
    x1_dev = t_dev(xo, y, c)
    c_dev = t_dev(xl, y, co)

    barrier = pltpu.get_barrier_semaphore()
    peers = [z_dev(d) for d in (8, -8, 4, -4, 2, -2, 1, -1)]
    peers += [x2_dev, x2_at(1), x2_at(-1), x1_dev, c_dev] + [t_dev(xl, y_at(d), c) for d in (1, 2, 3)]
    for peer in peers:
        pl.semaphore_signal(barrier, inc=1, device_id=peer, device_id_type=MESH)

    loads = []
    for i, (s, d) in enumerate(
        ((act_hbm, act_ref), (cot_hbm, cot_ref), (fold_hbm, fold_ref), (wg_hbm, wg), (wu_hbm, wu), (wd_hbm, wd),
         (unfold_hbm, unfold), (back_hbm, back), (last_hbm, last_ref))
    ):
        cp = pltpu.make_async_copy(s, d, local_sem.at[i])
        cp.start()
        loads.append(cp)

    sent = []

    def send(src, dst, dev):
        i = len(sent)
        cp = pltpu.make_async_remote_copy(
            src_ref=src, dst_ref=dst, send_sem=send_sem.at[i], recv_sem=recv_sem.at[i],
            device_id=dev, device_id_type=MESH,
        )
        cp.start()
        sent.append(cp)
        return cp

    stage16[...] = jnp.zeros_like(stage16)
    for cp in loads[:3]:
        cp.wait()
    stage16[0:TOK] = act_ref[...].astype(F32)
    stage16[8 : 8 + TOK] = cot_ref[...].astype(F32)
    raw = stage16[...].astype(BF16)
    block = jnp.zeros((ROWS, 128), F32)
    for q in range(QUARTERS):
        block += dot(fold_ref[q], raw[:, q * 128 : (q + 1) * 128])
    g_buf[0, 0, 0] = block.astype(BF16)

    pl.semaphore_wait(barrier, len(peers))

    own = g_buf.at[0, F0, 0]
    far = {}
    far[M8] = send(own, g_buf.at[0, M8, 0], z_dev(8))
    far[P8] = send(own, g_buf.at[0, P8, 0], z_dev(-8))
    far[M4] = send(own, g_buf.at[0, M4, 0], z_dev(4))
    far[P4] = send(own, g_buf.at[0, P4, 0], z_dev(-4))
    near, across = {}, {}

    def spread(f):
        block = g_buf.at[0, f, 0]
        near[f, 1] = send(block, g_buf.at[0, f, 1], z_dev(-1))
        near[f, 2] = send(block, g_buf.at[0, f, 2], z_dev(1))
        if f in ABOVE:
            near[f, 3] = send(block, g_buf.at[0, f, 3], z_dev(-2))
        for slot, source in BELOW.items():
            if source == f:
                near[slot, 3] = send(block, g_buf.at[0, slot, 3], z_dev(2))

    def cross(f):
        for w in (1, 2, 3):
            near[f, w].wait_recv()
        across[f] = send(g_buf.at[0, f], g_buf.at[1, f], x2_dev)

    def order(x, g):
        blocks = g_buf[x, 2 * g : 2 * g + 2].reshape(BLOCKS * ROWS, 128)
        for q in range(QUARTERS):
            rows = dot(unfold[q], blocks).astype(BF16)
            lanes = slice(q * 128, (q + 1) * 128)
            acts[x, g, :, lanes] = rows[:GROUP]
            cots[x, g, :, lanes] = rows[GROUP:]

    def order_other(g):
        across[2 * g].wait_recv()
        if g == 3:
            for cp in last:
                cp.wait_recv()
        else:
            across[2 * g + 1].wait_recv()
        order(1, g)

    spread(F0)
    far[P4].wait_recv()
    spread(P4)
    far[M4].wait_recv()
    spread(M4)
    far[M8].wait_recv()
    far[P8].wait_recv()
    odd = z % 2
    far[F16] = send(g_buf.at[0, M8 - odd, 0], g_buf.at[0, F16, 0], z_dev(8 + (zs - 16) * odd))
    far[M12] = send(g_buf.at[0, M8, 0], g_buf.at[0, M12, 0], z_dev(4))
    far[P12] = send(g_buf.at[0, P8, 0], g_buf.at[0, P12, 0], z_dev(-4))
    spread(P8)
    spread(M8)
    cross(F0)
    cross(P4)
    cross(M4)
    for cp in loads[3:]:
        cp.wait()
    order(0, 0)
    cross(P8)
    cross(M8)
    far[M12].wait_recv()
    spread(M12)
    far[P12].wait_recv()
    spread(P12)
    order(0, 1)
    far[F16].wait_recv()
    spread(F16)
    last = [
        send(g_buf.at[0, F16, 0], g_buf.at[1, F16, 0], x2_dev),
        send(g_buf.at[0, F16, 0], g_buf.at[1, F16, 1], x2_at(-1)),
        send(g_buf.at[0, F16, 0], g_buf.at[1, F16, 2], x2_at(1)),
    ]
    cross(P12)
    cross(M12)
    near[F16, 3].wait_recv()
    last.append(send(g_buf.at[0, F16, 3], g_buf.at[1, F16, 3], x2_dev))
    order(0, 2)
    order_other(0)
    near[F16, 1].wait_recv()
    near[F16, 2].wait_recv()
    order(0, 3)

    pair = {}

    def partial_sums(x):
        a_rows = acts[x].reshape(4 * GROUP, 512)
        c_rows = cots[x].reshape(4 * GROUP, 512)
        for j, (rows, weight) in enumerate(((a_rows, wg), (a_rows, wu), (c_rows, wd))):
            part = slice(j * GROUP, (j + 1) * GROUP)
            low = dot_t(rows, weight[0:256])
            high = dot_t(rows, weight[256:448])
            for f in range(4):
                r = slice(f * GROUP, (f + 1) * GROUP)
                pa[0, f, x, part] = low[r, 0:128]
                pb[0, x, f, part] = low[r, 128:256]
                pa[1, f, x, part] = high[r, 0:128]
                pb[1, x, f, part, 0:64] = high[r, 128:192]
                pb[1, x, f, part, 64:128] = jnp.zeros((GROUP, 64), F32)
        pair[x, 0] = send(pa.at[co, :, x], ra.at[:, x], c_dev)
        pair[x, 1] = send(pb.at[co, x], rb.at[x], c_dev)

    first_a = []

    def along_y(x):
        pair[x, 0].wait_recv()
        qa[:, x] = pa[c, :, x] + ra[:, x]
        for d in (2, 1, 3):
            dev = t_dev(xl, y_at(d), c)
            first_a.append(send(qa.at[y_at(d), x], a1.at[d - 1, x], dev))

    partial_sums(0)
    order_other(1)
    along_y(0)
    order_other(2)
    order_other(3)
    partial_sums(1)

    pair[0, 1].wait_recv()
    pair[1, 1].wait_recv()
    first_b, second_b = {}, []
    for d in (2, 1, 3, 0):
        r = y_at(d)
        qb[xo, r] = pb[c, xo, r] + rb[xo, r]
        first_b[d] = send(qb.at[xo, r], b1.at[r], x1_dev)
    along_y(1)
    qb[xl] = pb[c, xl] + rb[xl]
    for d in (2, 1, 3):
        r = y_at(d)
        first_b[d].wait_recv()
        sb[r] = qb[xl, r] + b1[r]
        second_b.append(send(sb.at[r], b2.at[d - 1], t_dev(xl, r, c)))
    for cp in first_a:
        cp.wait_recv()
    sa[xo] = qa[y, xo] + a1[0, xo] + a1[1, xo] + a1[2, xo]
    second_a = send(sa.at[xo], a2, x1_dev)
    sa[xl] = qa[y, xl] + a1[0, xl] + a1[1, xl] + a1[2, xl]
    first_b[0].wait_recv()
    sb[y] = qb[xl, y] + b1[y]

    def finish(sums):
        gate, up, grad = sums[0:GROUP], sums[GROUP : 2 * GROUP], sums[2 * GROUP : 3 * GROUP]
        s = jax.nn.sigmoid(gate)
        silu = gate * s
        hidden = (silu * up).astype(BF16)
        d_gate = (grad * up * s * (1.0 + gate * (1.0 - s))).astype(BF16)
        d_up = (grad * silu).astype(BF16)
        return jnp.concatenate([hidden, d_gate, d_up], axis=0)

    y_peers = [(d, t_dev(xl, y_at(d), c)) for d in (2, 1, 3)]
    cores = []
    second_a.wait_recv()
    ha[c, y, xl] = finish(sa[xl] + a2[...])
    near_a = send(ha.at[c, y, xl], ha.at[c, y, xl], x1_dev)
    for cp in second_b:
        cp.wait_recv()
    hb[c, xl, y] = finish(sb[y] + b2[0] + b2[1] + b2[2])
    near_b = [send(hb.at[c, xl, y], hb.at[c, xl, y], dev) for d, dev in y_peers]
    near_a.wait_recv()
    wide_a = [send(ha.at[c, y], ha.at[c, y], dev) for d, dev in y_peers]
    cores.append(send(ha.at[c, y], ha.at[c, y], c_dev))
    for cp in near_b:
        cp.wait_recv()
    wide_b = send(hb.at[c, xl], hb.at[c, xl], x1_dev)
    cores.append(send(hb.at[c, xl], hb.at[c, xl], c_dev))
    for (d, dev), cp in zip(y_peers, wide_a):
        cp.wait_recv()
        cores.append(send(ha.at[c, y_at(4 - d)], ha.at[c, y_at(4 - d)], c_dev))
    wide_b.wait_recv()
    cores.append(send(hb.at[c, xo], hb.at[c, xo], c_dev))
    def lay_out(half):
        low = pl.ds(pl.multiple_of(half * 256, 128), 128)
        high = pl.ds(pl.multiple_of(half * 256 + 128, 128), 128)
        for j in range(3):
            part = slice(j * GROUP, (j + 1) * GROUP)
            for x in range(2):
                for f in range(4):
                    hd[j, x, f, :, low] = ha[half, f, x, part]
                    hd[j, x, f, :, high] = hb[half, x, f, part]

    lay_out(c)
    for cp in cores:
        cp.wait_recv()
    lay_out(co)

    def hidden_sums(x):
        h, dg, du = [hd[j, x].reshape(4 * GROUP, 512)[:, :448] for j in range(3)]
        return dot(h, wd[...]), dot(dg, wg[...]) + dot(du, wu[...])

    over = {}

    def give(g):
        over[g] = send(xs.at[g], xr_buf.at[g], x2_dev)

    fwd, bwd = hidden_sums(1)
    for g in range(4):
        r = slice(g * GROUP, (g + 1) * GROUP)
        xs[g, 0:GROUP] = fwd[r].astype(BF16)
        xs[g, GROUP : 2 * GROUP] = bwd[r].astype(BF16)
    give(3)
    fwd, bwd = hidden_sums(0)
    give(2)
    for g in range(4):
        r = slice(g * GROUP, (g + 1) * GROUP)
        own_sum[g, 0:GROUP] = fwd[r]
        own_sum[g, GROUP : 2 * GROUP] = bwd[r]

    part_in = {}

    def collect(g):
        over[g].wait_recv()
        both = (own_sum[g] + xr_buf[g].astype(F32)).astype(BF16)
        rows = jnp.zeros((BLOCKS * ROWS, 128), F32)
        for q in range(QUARTERS):
            rows += dot(back[q], both[:, q * 128 : (q + 1) * 128])
        rows = rows.astype(BF16)
        for i in range(BLOCKS):
            rbuf[2 * g + i // 4, i % 4] = rows[i * ROWS : (i + 1) * ROWS]
        for f in (2 * g + 1, 2 * g):
            part_in[f, 0] = send(rbuf.at[f, 1], rw.at[f, 0], z_dev(1))
            part_in[f, 1] = send(rbuf.at[f, 2], rw.at[f, 1], z_dev(-1))
            if f in ABOVE:
                part_in[f, 2] = send(rbuf.at[f, 3], rw.at[f, 2], z_dev(2))
            else:
                part_in[BELOW[f], 3] = send(rbuf.at[f, 3], rw.at[BELOW[f], 3], z_dev(-2))

    def near_sum(f):
        total = rbuf[f, 0].astype(F32)
        for i in range(4):
            if (f, i) in part_in:
                part_in[f, i].wait_recv()
                total += rw[f, i].astype(F32)
        return total

    onward = {}

    def pass_on(i, f, dev, *others):
        total = near_sum(f)
        for o in others:
            onward[o].wait_recv()
            total += frecv[o].astype(F32)
        fsend[i] = total.astype(BF16)
        onward[i] = send(fsend.at[i], frecv.at[i], dev)

    stores = []

    def weight_grad(j, tokens, result):
        ref = grads.at[j]
        d = hd[j].reshape(8 * GROUP, 512)
        rows = tokens[...].reshape(8 * GROUP, 512)
        ref[0:256] = t_dot(d[:, 0:256], rows).astype(BF16)
        ref[256:448] = t_dot(d[:, 256:448], rows).astype(BF16)
        stores.append(pltpu.make_async_copy(ref, result, local_sem.at[9 + j]))
        stores[-1].start()

    weight_grad(1, acts, gg_hbm)
    collect(3)
    give(1)
    give(0)
    collect(2)
    pass_on(0, F16, z_dev(8))
    collect(1)
    pass_on(2, M12, z_dev(-4))
    pass_on(1, P12, z_dev(4))
    weight_grad(2, acts, gu_hbm)
    collect(0)
    pass_on(4, M8, z_dev(-8), 2)
    pass_on(3, P8, z_dev(8), 1, 0)
    pass_on(5, P4, z_dev(4))
    pass_on(6, M4, z_dev(-4))
    weight_grad(0, cots, gd_hbm)

    total = near_sum(F0)
    for o in (5, 6, 4, 3):
        onward[o].wait_recv()
        total += frecv[o].astype(F32)
    total = total.astype(BF16)
    for q in range(QUARTERS):
        stage16[:, q * 128 : (q + 1) * 128] = dot(last_ref[q], total)
    out_ref[...] = stage16[0:TOK].astype(BF16)
    gin_ref[...] = stage16[8 : 8 + TOK].astype(BF16)
    for cp in sent:
        cp.wait_send()
    for cp in stores:
        cp.wait()


def hand_over(*refs):
    sem = refs[-1]
    loads = [pltpu.make_async_copy(refs[i], refs[10 + i], sem.at[i]) for i in range(5)]
    stores = [pltpu.make_async_copy(refs[10 + i], refs[5 + i], sem.at[5 + i]) for i in range(5)]
    turns = (2, 3, 4, 0, 1)
    for i in turns:
        loads[i].start()
    for i in turns:
        loads[i].wait()
        stores[i].start()
    for i in turns:
        stores[i].wait()


def on_device(zs, activations, cotangent, w_gate, w_up, w_down):
    tokens, features = activations.shape
    hidden = w_gate.shape[0]
    fold, unfold, back, last = selections()
    vmem = pl.BlockSpec(memory_space=pltpu.VMEM)
    anywhere = pl.BlockSpec(memory_space=pl.ANY)
    weight = (hidden, features)
    row3 = 3 * GROUP
    scratch = [
        pltpu.VMEM((tokens, features), BF16), pltpu.VMEM((tokens, features), BF16),
        pltpu.VMEM(fold.shape, BF16), pltpu.VMEM(last.shape, BF16),
        pltpu.VMEM((3,) + weight, BF16),
        pltpu.VMEM(weight, BF16), pltpu.VMEM(weight, BF16), pltpu.VMEM(weight, BF16),
        pltpu.VMEM(unfold.shape, BF16), pltpu.VMEM(back.shape, BF16),
        pltpu.VMEM((16, features), F32),
        pltpu.VMEM((2, 8, 4, ROWS, 128), BF16),
        pltpu.VMEM((2, 4, GROUP, features), BF16), pltpu.VMEM((2, 4, GROUP, features), BF16),
        pltpu.VMEM((2, 4, 2, row3, 128), F32), pltpu.VMEM((2, 2, 4, row3, 128), F32),
        pltpu.VMEM((4, 2, row3, 128), F32), pltpu.VMEM((2, 4, row3, 128), F32),
        pltpu.VMEM((4, 2, row3, 128), F32), pltpu.VMEM((2, 4, row3, 128), F32),
        pltpu.VMEM((3, 2, row3, 128), F32), pltpu.VMEM((4, row3, 128), F32),
        pltpu.VMEM((2, row3, 128), F32), pltpu.VMEM((4, row3, 128), F32),
        pltpu.VMEM((row3, 128), F32), pltpu.VMEM((3, row3, 128), F32),
        pltpu.VMEM((2, 4, 2, row3, 128), BF16), pltpu.VMEM((2, 2, 4, row3, 128), BF16),
        pltpu.VMEM((3, 2, 4, GROUP, 512), BF16),
        pltpu.VMEM((4, 2 * GROUP, features), F32),
        pltpu.VMEM((4, 2 * GROUP, features), BF16), pltpu.VMEM((4, 2 * GROUP, features), BF16),
        pltpu.VMEM((8, 4, ROWS, 128), BF16), pltpu.VMEM((8, 4, ROWS, 128), BF16),
        pltpu.VMEM((7, ROWS, 128), BF16), pltpu.VMEM((7, ROWS, 128), BF16),
        pltpu.SemaphoreType.DMA((12,)),
        pltpu.SemaphoreType.DMA((N_COPIES,)), pltpu.SemaphoreType.DMA((N_COPIES,)),
    ]
    block = jax.ShapeDtypeStruct((tokens, features), BF16)
    grad = jax.ShapeDtypeStruct(weight, BF16)
    results = pl.pallas_call(
        functools.partial(kernel, zs),
        out_shape=(block, block, grad, grad, grad),
        in_specs=[anywhere] * 9,
        out_specs=(vmem,) * 2 + (anywhere,) * 3,
        scratch_shapes=scratch,
        compiler_params=pltpu.CompilerParams(
            collective_id=0, has_side_effects=True, vmem_limit_bytes=56 * 2**20
        ),
        cost_estimate=pl.CostEstimate(
            flops=18 * 384 * hidden * features, bytes_accessed=12 * hidden * features,
            transcendentals=0,
        ),
        name="ffn",
    )(activations, cotangent, w_gate, w_up, w_down, fold, unfold, back, last)
    return pl.pallas_call(
        hand_over,
        out_shape=(block, block, grad, grad, grad),
        in_specs=[anywhere] * 5,
        out_specs=(anywhere,) * 5,
        scratch_shapes=[pltpu.VMEM(v.shape, BF16) for v in results]
        + [pltpu.SemaphoreType.DMA((10,))],
        name="hand_over",
    )(*results)


def solution(mesh):
    spec = P("dp", "tensor")
    return jax.shard_map(
        functools.partial(on_device, mesh.shape["dp"] // 2),
        mesh=mesh,
        in_specs=(spec,) * 5,
        out_specs=(spec,) * 5,
        check_vma=False,
    )
```
